256 devices in a mesh: gx: 8 (over y, core), gy: 4 (over x), gz: 8 (over z).
Axes of the slice: x: 4, y: 4, z: 8, core: 2. Of those that a mesh axis runs over, the one named last changes fastest.
Arguments:
- offsets: float32 [3, 524288], P(None, ('gx', 'gy', 'gz')), may hold values from 0 to 1
- anchor: float32 [3, 524288], P(None, ('gx', 'gy', 'gz')), may hold values from 0 to 1
- stiffness: float32 [524288], P(('gx', 'gy', 'gz')), may hold values from 0.02 to 0.2
- lattice_block: int32 [524288, 1], P(('gx', 'gy', 'gz')), may hold values from 0 to 31; in each aligned block of 2048 rows (0 to 2047, 2048 to 4095, ...) at most 128 rows name the same one
- tile_ids: int32 [524288], P(('gx', 'gy', 'gz')), may hold values from 0 to 127
- populations: float32 [19, 64, 64, 1024], P(None, 'gx', 'gy', 'gz'), may hold values from 0 to 0.44, as said below
- visc_class: int32 [64, 64, 1024], P('gx', 'gy', 'gz'), may hold values from 0 to 3
- fluid_mask: int32 [64, 64, 1024], P('gx', 'gy', 'gz'), may hold values 0 or 1
- tau_table: float32 [4], replicated, may hold values from 0.55 to 1.5
Outputs:
- new_populations: float32 [19, 64, 64, 1024], P(None, 'gx', 'gy', 'gz')
- vertex_velocity: float32 [3, 524288], P(None, ('gx', 'gy', 'gz'))
The draws below stay inside these ranges and needn't reach their ends.
Inputs may be any that keep to these rules, and one draw needn't show every extreme that they name: `lattice_block`: at most 128 vertices of one cell block name the same lattice brick, and in every draw some brick is named by exactly 128 vertices of some block. `populations`: each distribution lies between 0.7 and 1.3 times its lattice weight.
All inputs are finite; a program needn't handle non-finite values. No bound on the sum of `fluid_mask` on one device may be relied on, other than what follows from the above.
Results may differ from the reference program's by a relative error of at most 0.0003.
Values sent between devices are 32-bit elements; how exact they have to be, the bound alone decides.
A program may use at most 128 MiB of HBM per device.

```python
import math
import jax
import jax.numpy as jnp
import numpy as np
from jax import lax

BX = 8
BY = 16
BZ = 128
VDEV = 2048
CAP = 128
NCLASS = 4
NX = 64
NY = 64
NZ = 1024
VERTS = 524288
NTILE = 128
N_GY = 4
N_GZ = 8


lattice_weight = [1.0 / 3.0] + [1.0 / 18.0] * 6 + [1.0 / 36.0] * 12


def draw_populations(key, part):
    key = jax.random.fold_in(key, 11)
    weights = jnp.array(lattice_weight, jnp.float32)
    noise = jax.random.uniform(key, (19, NX, NY, NZ), jnp.float32, 0.7, 1.3)
    return weights[:, None, None, None] * noise


def plant(drawn, key, least, largest):
    place = [jax.random.randint(jax.random.fold_in(key, axis), (), 0, length) for axis, length in enumerate(drawn.shape)]
    main_axis = drawn.shape.index(max(drawn.shape))
    next_to = place[:main_axis] + [(place[main_axis] + 1) % drawn.shape[main_axis]] + place[main_axis + 1:]
    return drawn.at[tuple(place)].set(least).at[tuple(next_to)].set(largest)


def level_of(own_key, dims, shards, smallest, top_value):
    loudness = 1.0
    for axis_at, blocks in shards:
        steps = jax.random.uniform(jax.random.fold_in(jax.random.fold_in(own_key, 6), axis_at), (blocks,), jnp.float32, smallest / len(shards), top_value / len(shards))
        loudness = loudness * jnp.repeat(jnp.exp(steps), dims[axis_at] // blocks).reshape((-1,) + (1,) * (len(dims) - 1 - axis_at))
    return loudness


def shared_out(rng, own, number, rows, count, top, limit, lean):
    sequence = jax.random.permutation(rng, count)
    crowded, ordinary = shares(count, rows * top, limit, lean, True), shares(count, rows * top, limit, lean, False)
    places = jnp.arange(count)

    def named(sizes, offset_by):
        used = int((sizes > 0).sum())
        fixed = max(1, used // 4)
        moved = fixed + (places - fixed + offset_by * (used - fixed)) % max(1, count - fixed)
        return jnp.zeros((count,), jnp.int32).at[sequence[jnp.where(places < fixed, places, moved)]].set(jnp.asarray(sizes, jnp.int32))

    sizes = jnp.where(number % 4 == 0, named(crowded, number // 4), named(ordinary, number - number // 4 - 1))
    mixed = jax.random.permutation(jax.random.fold_in(own, 3), count)
    source_of, receiver = mixed[0:count // 2 * 2:2], mixed[1:count // 2 * 2:2]
    margin = jnp.minimum(sizes[source_of] - 1, limit - sizes[receiver]) // 2
    margin = jnp.where((source_of == sequence[0]) | (receiver == sequence[0]) | (sizes[receiver] == 0), 0, jnp.maximum(margin, 0))
    moved = jax.random.randint(jax.random.fold_in(own, 4), (count // 2,), 0, 1 << 20) % (margin + 1)
    sizes = sizes.at[source_of].add(-moved).at[receiver].add(moved)
    items = jnp.searchsorted(jnp.cumsum(sizes), jnp.arange(rows * top), side="right").astype(jnp.int32)
    table = items.reshape(top, rows).T
    table = table[jax.random.permutation(jax.random.fold_in(own, 1), rows)]
    offset_by = jax.random.randint(jax.random.fold_in(own, 2), (rows, 1), 0, top)
    return jnp.take_along_axis(table, (jnp.arange(top)[None, :] + offset_by) % top, axis=1)


def shares(amount, total, limit, skew, full):
    weights = [(1 << 20) // math.isqrt(standing ** skew) + 1 for standing in range(1, amount + 1)]
    largest = limit if full else min(limit, max(-(-total // amount), total * weights[0] // sum(weights)))
    least = 1 if total - largest >= amount - 1 else 0
    counts, rest = [largest] + [least] * (amount - 1), total - largest - least * (amount - 1)
    while rest > 0:
        candidates = [i for i in range(1, amount) if counts[i] < largest] or [i for i in range(1, amount) if counts[i] < limit]
        pool, remaining = sum([weights[i] for i in candidates]), rest
        for i in candidates:
            addition = min(limit - counts[i], max(1, remaining * weights[i] // pool), rest)
            counts[i] = counts[i] + addition
            rest = rest - addition
    return np.array(counts)


def setup_inputs(seed: int = 0) -> dict:
    key_of = jax.random.split(jax.random.key(seed), 10)
    offsets = jnp.clip(1.0 * jax.random.uniform(key_of[0], (3, VERTS), jnp.float32) ** level_of(key_of[0], (3, VERTS), ((1, 256),), -0.2, 0.2), 0.0, 1.0)
    anchor = jnp.clip(1.0 * jax.random.uniform(key_of[1], (3, VERTS), jnp.float32) ** level_of(key_of[1], (3, VERTS), ((1, 256),), -0.2, 0.2), 0.0, 1.0)
    stiffness = jnp.clip(jnp.exp(math.log(0.2) - 2.3025851 * jax.random.uniform(key_of[2], (VERTS,), jnp.float32) ** level_of(key_of[2], (VERTS,), ((0, 256),), -0.2, 0.2)), 0.02, 0.2)
    lattice_block_keys = jax.random.split(jax.random.fold_in(key_of[3], 1), VERTS // VDEV)
    lattice_block_turns = jax.random.permutation(jax.random.fold_in(key_of[3], 3), VERTS // VDEV)
    lattice_block = jax.vmap(lambda own, number: shared_out(jax.random.fold_in(key_of[3], 2), own, number, VDEV, N_GY * N_GZ, 1, CAP, 2))(lattice_block_keys, lattice_block_turns).reshape((VERTS, 1))
    tile_ids = plant(jax.random.randint(key_of[4], (VERTS,), 0, NTILE), jax.random.fold_in(key_of[4], 1), 0, NTILE - 1).astype(jnp.int32)
    populations = draw_populations(jax.random.fold_in(key_of[9], 71), 0)
    visc_class = plant(jax.random.randint(key_of[6], (NX, NY, NZ), 0, NCLASS), jax.random.fold_in(key_of[6], 1), 0, NCLASS - 1).astype(jnp.int32)
    fluid_mask = plant((jax.random.randint(key_of[7], (NX, NY, NZ), 0, 8) < 7).astype(jnp.int32), jax.random.fold_in(key_of[7], 1), 0, 1)
    tau_table = jnp.clip(jax.random.uniform(key_of[8], (NCLASS,), jnp.float32, 0.55, 1.5), 0.55, 1.5)
    return dict(offsets=offsets, anchor=anchor, stiffness=stiffness, lattice_block=lattice_block, tile_ids=tile_ids, populations=populations, visc_class=visc_class, fluid_mask=fluid_mask, tau_table=tau_table)


lattice_velocity = [(0, 0, 0), (1, 0, 0), (-1, 0, 0), (0, 1, 0), (0, -1, 0), (0, 0, 1), (0, 0, -1),
                    (1, 1, 0), (-1, -1, 0), (1, -1, 0), (-1, 1, 0), (1, 0, 1), (-1, 0, -1),
                    (1, 0, -1), (-1, 0, 1), (0, 1, 1), (0, -1, -1), (0, 1, -1), (0, -1, 1)]
lattice_weight = [1.0 / 3.0] + [1.0 / 18.0] * 6 + [1.0 / 36.0] * 12
opposite = [0, 2, 1, 4, 3, 6, 5, 8, 7, 10, 9, 12, 11, 14, 13, 16, 15, 18, 17]
speed_scale = 20.0


def tent_weight(distance, radius):
    return jnp.maximum(0.0, 1.0 - jnp.abs(distance) / radius)


def tile_weights(offsets):
    site = jnp.arange(128)
    coord_a = (site // 64).astype(jnp.float32)
    coord_b = ((site // 32) % 2).astype(jnp.float32)
    coord_c = (site % 32).astype(jnp.float32)
    return (tent_weight(2.0 * offsets[0][:, None] - coord_a[None, :], 1.5)
            * tent_weight(2.0 * offsets[1][:, None] - coord_b[None, :], 1.5)
            * tent_weight(32.0 * offsets[2][:, None] - coord_c[None, :], 2.0))


def moment_of(values, axis_pick):
    total = jnp.zeros_like(values[0])
    for index in range(19):
        coefficient = lattice_velocity[index][axis_pick]
        if coefficient != 0:
            total = total + coefficient * values[index]
    return total


def velocity(populations, force_field):
    density = jnp.sum(populations, axis=0)
    return jnp.stack([(moment_of(populations, axis_pick) + 0.5 * force_field[axis_pick]) / density
                      for axis_pick in range(3)])


def collide(populations, force_field, relax_time, fluid_flag):
    density = jnp.sum(populations, axis=0)
    flow = [(moment_of(populations, axis_pick) + 0.5 * force_field[axis_pick]) / density
            for axis_pick in range(3)]
    speed_sq = flow[0] * flow[0] + flow[1] * flow[1] + flow[2] * flow[2]
    work_rate = flow[0] * force_field[0] + flow[1] * force_field[1] + flow[2] * force_field[2]
    inverse = 1.0 / relax_time
    source_gain = 1.0 - 0.5 * inverse
    result = []
    for index in range(19):
        proj_u = jnp.zeros_like(density)
        proj_f = jnp.zeros_like(density)
        for axis_pick in range(3):
            coefficient = lattice_velocity[index][axis_pick]
            if coefficient != 0:
                proj_u = proj_u + coefficient * flow[axis_pick]
                proj_f = proj_f + coefficient * force_field[axis_pick]
        weight = lattice_weight[index]
        equilib = weight * density * (1.0 + 3.0 * proj_u + 4.5 * proj_u * proj_u - 1.5 * speed_sq)
        source = source_gain * weight * (3.0 * (proj_f - work_rate) + 9.0 * proj_u * proj_f)
        collided = populations[index] - (populations[index] - equilib) * inverse + source
        result.append(jnp.where(fluid_flag > 0.5, collided, populations[opposite[index]]))
    return jnp.stack(result)


def reference(offsets, anchor, stiffness, lattice_block, tile_ids, populations, visc_class, fluid_mask, tau_table):
    vertex_force = stiffness[None, :] * (anchor - offsets)
    groups = N_GY * N_GZ
    tiles_x, tiles_y, tiles_z = BX // 2, BY // 2, BZ // 32
    grid_x, grid_y, grid_z = NX // 2, NY // 2, NZ // 32
    verts = offsets.shape[1]
    vertex_id = jnp.arange(verts).astype(jnp.int32)
    slab_index = vertex_id // (VDEV * groups)
    target = lattice_block[:, 0]
    block_y = target // N_GZ
    block_z = target % N_GZ
    tile_x = tile_ids // (tiles_y * tiles_z)
    tile_y = (tile_ids // tiles_z) % tiles_y
    tile_z = tile_ids % tiles_z
    global_tile = (((slab_index * tiles_x + tile_x) * grid_y + block_y * tiles_y + tile_y) * grid_z
                   + block_z * tiles_z + tile_z).astype(jnp.int32)
    block_rows = math.gcd(verts, 16384)
    block_count = verts // block_rows
    off_blocks = offsets.reshape(3, block_count, block_rows).transpose(1, 0, 2)
    force_blocks = vertex_force.reshape(3, block_count, block_rows).transpose(1, 0, 2)
    tile_blocks = global_tile.reshape(block_count, block_rows)

    def spread_block(tile_grid, pieces):
        off_piece, force_piece, tile_piece = pieces
        weights = tile_weights(off_piece)
        contribution = (weights[:, None, :] * force_piece.T[:, :, None]).reshape(block_rows, 384)
        return tile_grid.at[tile_piece].add(contribution), None

    tile_grid = jnp.zeros((grid_x * grid_y * grid_z, 384), jnp.float32)
    tile_grid, unused = lax.scan(spread_block, tile_grid, (off_blocks, force_blocks, tile_blocks))
    force_field = tile_grid.reshape(grid_x, grid_y, grid_z, 3, 2, 2, 32).transpose(3, 0, 4, 1, 5, 2, 6).reshape(3, NX, NY, NZ)
    relax_time = jnp.zeros(visc_class.shape, jnp.float32)
    for klass in range(NCLASS):
        relax_time = relax_time + jnp.where(visc_class == klass, tau_table[klass], 0.0)
    fluid_flag = fluid_mask.astype(jnp.float32)
    current = populations
    for sweep_idx in range(2):
        collided = collide(current, force_field, relax_time, fluid_flag)
        current = jnp.stack([jnp.roll(collided[index], lattice_velocity[index], axis=(0, 1, 2)) for index in range(19)])
    flow_field = velocity(current, force_field)
    flow_tiles = flow_field.reshape(3, grid_x, 2, grid_y, 2, grid_z, 32).transpose(1, 3, 5, 0, 2, 4, 6).reshape(-1, 384)

    def sample_block(carry, pieces):
        off_piece, tile_piece = pieces
        weights = tile_weights(off_piece)
        gathered = flow_tiles[tile_piece].reshape(block_rows, 3, 128)
        return carry, speed_scale * jnp.sum(gathered * weights[:, None, :], axis=2)

    unused, sampled = lax.scan(sample_block, 0.0, (off_blocks, tile_blocks))
    vertex_velocity = sampled.transpose(2, 0, 1).reshape(3, verts)
    return current, vertex_velocity
```

```python
import functools

import jax
import jax.numpy as jnp
from jax import lax
from jax.experimental import pallas as pl
from jax.experimental.pallas import tpu as pltpu
from jax.sharding import PartitionSpec as P

MESH = pl.DeviceIdType.MESH
CAP = 128
BX, BY, BZ = 8, 16, 128
SITES = BX * BY
XPAD, YPAD = BX + 2, 32
F32, BF16, I32 = jnp.float32, jnp.bfloat16, jnp.int32

lattice_velocity = [
    (0, 0, 0),
    (1, 0, 0),
    (-1, 0, 0),
    (0, 1, 0),
    (0, -1, 0),
    (0, 0, 1),
    (0, 0, -1),
    (1, 1, 0),
    (-1, -1, 0),
    (1, -1, 0),
    (-1, 1, 0),
    (1, 0, 1),
    (-1, 0, -1),
    (1, 0, -1),
    (-1, 0, 1),
    (0, 1, 1),
    (0, -1, -1),
    (0, 1, -1),
    (0, -1, 1),
]
lattice_weight = [1.0 / 3.0] + [1.0 / 18.0] * 6 + [1.0 / 36.0] * 12
speed_scale = 20.0
pairs = [(i, i + 1) for i in range(1, 19, 2)]


def crossing(axis, sign):
    return [i for i in range(19) if lattice_velocity[i][axis] == sign]


XSET = [crossing(0, 1), crossing(0, -1)]
YSET = [crossing(1, 1), crossing(1, -1)]
ZSET = [crossing(2, 1), crossing(2, -1)]


def dist_of(*velocity):
    return lattice_velocity.index(tuple(velocity))


def z_lane(side, index, x):
    return ZSET[side].index(index) * XPAD + x + 1


def row_of(index, x, y):
    return (index * XPAD + x + 1) * YPAD + 8 + y


def moments(f, force):
    density = functools.reduce(lambda a, b: a + b, f)
    inverse = 1.0 / density
    flow = []
    for axis in range(3):
        plus = [f[i] for i in crossing(axis, 1)]
        minus = [f[i] for i in crossing(axis, -1)]
        total = functools.reduce(lambda a, b: a + b, plus) - functools.reduce(lambda a, b: a + b, minus)
        flow.append((total + 0.5 * force[axis]) * inverse)
    return density, flow


def collide(f, force, omega, fluid):
    density, flow = moments(f, force)
    speed_sq = flow[0] * flow[0] + flow[1] * flow[1] + flow[2] * flow[2]
    work = flow[0] * force[0] + flow[1] * force[1] + flow[2] * force[2]
    gain = 1.0 - 0.5 * omega
    keep = 1.0 - omega
    amount = omega * density
    base = amount * (1.0 - 1.5 * speed_sq) - (3.0 * gain) * work
    momentum = [amount * flow[a] for a in range(3)]
    push = [gain * force[a] for a in range(3)]
    steep = [4.5 * momentum[a] + 9.0 * push[a] for a in range(3)]
    slope = [3.0 * (momentum[a] + push[a]) for a in range(3)]
    result = [None] * 19
    result[0] = jnp.where(fluid, keep * f[0] + lattice_weight[0] * base, f[0])

    def along(values, velocity):
        total = None
        for axis in range(3):
            if velocity[axis]:
                if total is None:
                    total = values[axis] if velocity[axis] > 0 else -values[axis]
                else:
                    total = total + values[axis] if velocity[axis] > 0 else total - values[axis]
        return total

    for i, j in pairs:
        velocity = lattice_velocity[i]
        even = base + along(flow, velocity) * along(steep, velocity)
        odd = along(slope, velocity)
        weight = lattice_weight[i]
        result[i] = jnp.where(fluid, keep * f[i] + weight * (even + odd), f[j])
        result[j] = jnp.where(fluid, keep * f[j] + weight * (even - odd), f[i])
    return result


def kernel(
    sizes,
    off_ref,
    anc_ref,
    stf_ref,
    tgt_ref,
    tid_ref,
    tau_ref,
    pop_hbm,
    cls_hbm,
    flu_hbm,
    out_hbm,
    vel_ref,
    pops,
    cls,
    flu,
    rows,
    rt,
    lhs,
    outbuf,
    inbuf,
    wz,
    wxy,
    load,
    acc,
    force,
    field,
    xs,
    xr,
    ys,
    yr,
    xyr,
    zs,
    zr,
    xzr,
    yzr,
    zp,
    ubuf,
    newp,
    vbuf,
    ret,
    in_sem,
    out_sem,
    fwd_send,
    fwd_recv,
    halo_send,
    halo_recv,
    back_send,
    back_recv,
):
    n_gx, n_gy, n_gz = sizes
    groups = n_gy * n_gz
    verts = off_ref.shape[1]
    chunks = verts // 128
    gx, gy, gz = lax.axis_index("gx"), lax.axis_index("gy"), lax.axis_index("gz")

    def device(dx, dy, dz):
        return (
            lax.rem(gx + dx + n_gx, n_gx),
            lax.rem(gy + dy + n_gy, n_gy),
            lax.rem(gz + dz + n_gz, n_gz),
        )

    loads = [
        pltpu.make_async_copy(pop_hbm, pops, in_sem.at[0]),
        pltpu.make_async_copy(cls_hbm, cls, in_sem.at[1]),
        pltpu.make_async_copy(flu_hbm, flu, in_sem.at[2]),
    ]
    for copy in loads:
        copy.start()

    barrier = pltpu.get_barrier_semaphore()

    @pl.loop(1, groups)
    def _(d):
        pl.semaphore_signal(
            barrier, inc=1, device_id=device(0, d // n_gz, lax.rem(d, n_gz)), device_id_type=MESH
        )

    others = [(sx, 0, 0) for sx in (1, -1)]
    others += [(sx, sy, 0) for sx in (1, -1) for sy in (1, -1)]
    others += [(sx, 0, sz) for sx in (1, -1) for sz in (1, -1)]
    for offset in others:
        pl.semaphore_signal(barrier, inc=1, device_id=device(*offset), device_id_type=MESH)

    target = tgt_ref[...]
    rel_y = lax.rem(target // n_gz - gy + n_gy, n_gy)
    rel_z = lax.rem(lax.rem(target, n_gz) - gz + n_gz, n_gz)
    rel = rel_y * n_gz + rel_z
    member = rel == lax.broadcasted_iota(I32, (groups, verts), 0)
    member_f = jnp.where(member, 1.0, 0.0).astype(F32)
    stacked = jnp.concatenate([member_f[:, c * 128 : (c + 1) * 128] for c in range(chunks)], axis=0)
    row_id = lax.broadcasted_iota(I32, (128, 256), 0)
    col_id = lax.broadcasted_iota(I32, (128, 256), 1)
    prefix = jnp.where((row_id < col_id) | (col_id >= 128), 1.0, 0.0).astype(BF16)
    counts = jnp.dot(stacked.astype(BF16), prefix, preferred_element_type=F32)
    base = jnp.zeros((groups, 128), F32)
    slot_id = lax.broadcasted_iota(I32, (128, 128), 0).astype(F32)
    for c in range(chunks):
        part = counts[c * groups : (c + 1) * groups]
        rank = jnp.sum(
            member_f[:, c * 128 : (c + 1) * 128] * (part[:, :128] + base), axis=0, keepdims=True
        )
        base = base + part[:, 128:]
        rt[:, c * 128 : (c + 1) * 128] = jnp.where(rank == slot_id, 1.0, 0.0).astype(BF16)

    def high(value):
        return value.astype(BF16).astype(F32)

    offs = off_ref[...]
    push = stf_ref[...] * (anc_ref[...] - offs)
    offs_hi = high(offs)
    offs_mid = high(offs - offs_hi)
    push_hi = high(push)
    rows[...] = jnp.zeros((16, verts), F32)
    rows[0:3, :] = offs_hi
    rows[3:6, :] = push_hi
    rows[6:7, :] = tid_ref[...].astype(F32)
    rows[7:8, :] = (offs - offs_hi - offs_mid)[2:3]
    rows[8:11, :] = offs_mid
    rows[11:14, :] = push - push_hi
    for d in range(groups):
        lhs[d * 16 : (d + 1) * 16, :] = jnp.where(rel == d, rows[...], 0.0).astype(BF16)
    packed = lax.dot_general(
        lhs[...], rt[...], (((1,), (1,)), ((), ())), preferred_element_type=F32
    )
    sub8 = lax.broadcasted_iota(I32, (8, 128), 0)
    lane8 = lax.broadcasted_iota(I32, (8, 128), 1)
    for d in range(groups):
        both = packed[d * 16 : d * 16 + 8] + packed[d * 16 + 8 : d * 16 + 16]
        fine = pltpu.roll(both, 3, axis=0)
        outbuf[d] = both + jnp.where(sub8 == 2, fine, 0.0)
    inbuf[0] = outbuf[0]

    pl.semaphore_wait(barrier, groups - 1 + len(others))

    def forward(d):
        return pltpu.make_async_remote_copy(
            src_ref=outbuf.at[d],
            dst_ref=inbuf.at[d],
            send_sem=fwd_send.at[d],
            recv_sem=fwd_recv.at[d],
            device_id=device(0, d // n_gz, lax.rem(d, n_gz)),
            device_id_type=MESH,
        )

    @pl.loop(1, groups)
    def _(d):
        forward(d).start()

    x_id = lax.broadcasted_iota(I32, (BX, 128), 0)
    y_id = lax.broadcasted_iota(I32, (BY, 128), 0)
    z_id = lax.broadcasted_iota(I32, (BZ, 128), 0)
    z_half = 0.5 * z_id.astype(F32)

    def spread(d):
        blk = inbuf[d]
        tile = blk[6:7].astype(I32)
        tile_x, tile_y, tile_z = tile // 32, lax.rem(tile // 4, 8), lax.rem(tile, 4)
        dist_x = 2.0 * blk[0:1] - (x_id - 2 * tile_x).astype(F32)
        wx = jnp.where(x_id // 2 == tile_x, jnp.maximum(0.0, 1.0 - jnp.abs(dist_x) * (1.0 / 1.5)), 0.0)
        dist_y = 2.0 * blk[1:2] - (y_id - 2 * tile_y).astype(F32)
        wy = jnp.where(y_id // 2 == tile_y, jnp.maximum(0.0, 1.0 - jnp.abs(dist_y) * (1.0 / 1.5)), 0.0)
        place = 16.0 * blk[2:3] + 16.0 * tile_z.astype(F32)
        weight = jnp.where(z_id // 32 == tile_z, jnp.maximum(0.0, 1.0 - jnp.abs(place - z_half)), 0.0)
        lanes = pl.ds(pl.multiple_of(d * 128, 128), 128)
        weight_hi = weight.astype(BF16)
        wz[0:BZ, lanes] = weight_hi
        wz[BZ : 2 * BZ, lanes] = (weight - weight_hi.astype(F32)).astype(BF16)
        for x in range(BX):
            plane = wx[x : x + 1] * wy
            wxy[x * BY : (x + 1) * BY, lanes] = plane
            for c in range(3):
                value = plane * blk[3 + c : 4 + c]
                value_hi = value.astype(BF16)
                at = c * SITES + x * BY
                load[at : at + BY, lanes] = value_hi
                at += 3 * SITES
                load[at : at + BY, lanes] = (value - value_hi.astype(F32)).astype(BF16)

    per = 8
    for part in range(groups // per):

        @pl.loop(part * per, (part + 1) * per)
        def _(d):
            @pl.when(d > 0)
            def _():
                forward(d).wait_recv()

            spread(d)

        span = slice(part * per * 128, (part + 1) * per * 128)
        product = lax.dot_general(
            load[:, span], wz[:, span], (((1,), (1,)), ((), ())), preferred_element_type=F32
        )
        if part == 0:
            acc[...] = product
        else:
            acc[...] += product
    half = 3 * SITES
    force[...] = (acc[0:half, 0:128] + acc[0:half, 128:256]) + (
        acc[half : 2 * half, 0:128] + acc[half : 2 * half, 128:256]
    )

    for copy in loads:
        copy.wait()

    taus = [1.0 / jnp.full((8, 128), tau_ref[k], F32) for k in range(4)]

    def site_values(x, h):
        rows_at = pl.ds(8 * h, 8)
        klass = cls[x, rows_at, :]
        omega = jnp.where(
            klass < 2, jnp.where(klass == 0, taus[0], taus[1]), jnp.where(klass == 2, taus[2], taus[3])
        )
        return omega, flu[x, rows_at, :] > 0

    def forces(x, h):
        return [
            force[pl.ds(pl.multiple_of(c * SITES + x * BY + 8 * h, 8), 8), :] for c in range(3)
        ]

    def messages(p):
        found = []
        for s, sign in enumerate((1, -1)):
            found.append(((sign, 0, 0), xs.at[p, s], xr.at[p, s]))
            found.append(((0, sign, 0), ys.at[p, s], yr.at[p, s]))
            found.append(((0, 0, sign), zs.at[p, s], zr.at[p, s]))
            for t, other in enumerate((1, -1)):
                spot = YSET[s].index(dist_of(other, sign, 0))
                found.append(((other, sign, 0), ys.at[p, s, spot], xyr.at[p, s, t]))
                found.append(((other, 0, sign), zs.at[p, s], xzr.at[p, s, t]))
                edge = pl.ds(8 if other > 0 else 0, 8)
                found.append(((0, other, sign), zs.at[p, s, edge], yzr.at[p, s, t]))
        return found

    def halo(p):
        return [
            pltpu.make_async_remote_copy(
                src_ref=src,
                dst_ref=dst,
                send_sem=halo_send.at[p, m],
                recv_sem=halo_recv.at[p, m],
                device_id=device(*offset),
                device_id_type=MESH,
            )
            for m, (offset, src, dst) in enumerate(messages(p))
        ]

    def streamed(p, x, h):
        found = []
        for i in range(19):
            cx, cy, cz = lattice_velocity[i]
            start = row_of(i, x - cx, 8 * h - cy)
            if cy == 0:
                start = pl.multiple_of(start, 8)
            value = field[p, pl.ds(start, 8), :]
            if cz:
                s = 0 if cz > 0 else 1
                border = zp[p, s, 8 + 8 * h - cy : 16 + 8 * h - cy, :]
                lane = z_lane(s, i, x - cx)
                edge = 0 if cz > 0 else 127
                shift = 128 - lane if cz > 0 else 127 - lane
                value = jnp.where(
                    lane8 == edge,
                    pltpu.roll(border, shift, axis=1),
                    pltpu.roll(value, 1 if cz > 0 else 127, axis=1),
                )
            found.append(value)
        return found

    def sweep(p, source):
        def body(x, borders):
            borders = list(borders)
            for h in range(2):
                omega, fluid = site_values(x, h)
                result = collide(source(x, h), forces(x, h), omega, fluid)
                for i in range(19):
                    field[p, pl.ds(pl.multiple_of(row_of(i, x, 8 * h), 8), 8), :] = result[i]
                for s in range(2):
                    for i in ZSET[s]:
                        lane = z_lane(s, i, x)
                        shift = lane + 1 if s == 0 else lane
                        borders[2 * s + h] = jnp.where(
                            lane8 == lane, pltpu.roll(result[i], shift, axis=1), borders[2 * s + h]
                        )
            return tuple(borders)

        zero = jnp.zeros((8, 128), F32)
        borders = lax.fori_loop(0, BX, body, (zero, zero, zero, zero))
        for s in range(2):
            for h in range(2):
                zs[p, s, 8 * h : 8 * h + 8, :] = borders[2 * s + h]
            for k, i in enumerate(YSET[s]):
                ys[p, s, k] = field[p, pl.ds(row_of(i, 0, BY - 1 if s == 0 else 0), BX, stride=YPAD), :]
            for k, i in enumerate(XSET[s]):
                start = row_of(i, BX - 1 if s == 0 else 0, 0)
                xs[p, s, k] = field[p, start : start + BY, :]
        copies = halo(p)
        for copy in copies:
            copy.start()
        for copy in copies:
            copy.wait_recv()
        lane16 = lax.broadcasted_iota(I32, (BY, 128), 1)
        for s, sign in enumerate((1, -1)):
            for k, i in enumerate(XSET[s]):
                start = row_of(i, -1 if s == 0 else BX, 0)
                field[p, start : start + BY, :] = xr[p, s, k]
            for k, i in enumerate(YSET[s]):
                field[p, pl.ds(row_of(i, 0, -1 if s == 0 else BY), BX, stride=YPAD), :] = yr[p, s, k]
            plane = zr[p, s]
            for t, other in enumerate((1, -1)):
                i = dist_of(other, sign, 0)
                start = row_of(i, -1 if other > 0 else BX, -1 if s == 0 else BY)
                row = BX - 1 if other > 0 else 0
                field[p, start : start + 1, :] = xyr[p, s, t, row : row + 1, :]
                i = dist_of(other, 0, sign)
                lane = z_lane(s, i, -1 if other > 0 else BX)
                shift = 128 - BX if other > 0 else BX
                plane = jnp.where(lane16 == lane, pltpu.roll(xzr[p, s, t], shift, axis=1), plane)
                to, row = (7, 7) if other > 0 else (24, 0)
                zp[p, s, to : to + 1, :] = yzr[p, s, t, row : row + 1, :]
            zp[p, s, 8:24, :] = plane
        return copies

    def first(x, h):
        return [pops[i, x, pl.ds(8 * h, 8), :] for i in range(19)]

    sent = sweep(0, first)
    sent += sweep(1, functools.partial(streamed, 0))

    @pl.loop(0, BX)
    def _(x):
        for h in range(2):
            result = streamed(1, x, h)
            for i in range(19):
                newp[i, x, pl.ds(8 * h, 8), :] = result[i]
            density, flow = moments(result, forces(x, h))
            for c in range(3):
                ubuf[pl.ds(pl.multiple_of(c * SITES + x * BY + 8 * h, 8), 8), :] = flow[c]

    store = pltpu.make_async_copy(newp, out_hbm, out_sem)
    store.start()

    flow = ubuf[...]
    flow_hi = flow.astype(BF16)
    flow_lo = (flow - flow_hi.astype(F32)).astype(BF16)
    flow_all = jnp.concatenate([flow_hi, flow_hi, flow_lo, flow_lo], axis=1)

    def backward(d):
        return pltpu.make_async_remote_copy(
            src_ref=vbuf.at[pl.ds(pl.multiple_of(d * 8, 8), 8)],
            dst_ref=ret.at[pl.ds(pl.multiple_of(d * 8, 8), 8)],
            send_sem=back_send.at[d],
            recv_sem=back_recv.at[d],
            device_id=device(0, -(d // n_gz), -lax.rem(d, n_gz)),
            device_id_type=MESH,
        )

    @pl.loop(0, groups // 2)
    def _(pair):
        lanes = pl.ds(pl.multiple_of(pair * 256, 256), 256)
        block = wz[:, lanes]
        picked = jnp.dot(
            flow_all, jnp.concatenate([block, block], axis=0), preferred_element_type=F32
        )
        plane = wxy[:, lanes]
        for c in range(3):
            speed = speed_scale * jnp.sum(
                picked[c * SITES : (c + 1) * SITES] * plane, axis=0, keepdims=True
            )
            for e in range(2):
                vbuf[pl.ds(pair * 16 + 8 * e + c, 1), :] = speed[:, e * 128 : (e + 1) * 128]
        for e in range(2):
            d = pair * 2 + e

            @pl.when(d > 0)
            def _():
                backward(d).start()

    ret[0:8, :] = vbuf[0:8, :]

    @pl.loop(1, groups)
    def _(d):
        backward(d).wait_recv()

    answer = jnp.concatenate([ret[pl.ds(c, groups, stride=8), :] for c in range(3)], axis=0)
    answer_hi = answer.astype(BF16)
    answer_lo = (answer - answer_hi.astype(F32)).astype(BF16)
    found = jnp.dot(
        jnp.concatenate([answer_hi, answer_lo], axis=0), rt[...], preferred_element_type=F32
    )
    found = found[0 : 3 * groups] + found[3 * groups :]
    for c in range(3):
        vel_ref[c : c + 1, :] = jnp.sum(
            jnp.where(member, found[c * groups : (c + 1) * groups], 0.0), axis=0, keepdims=True
        )

    for copy in sent:
        copy.wait_send()

    @pl.loop(1, groups)
    def _(d):
        forward(d).wait_send()
        backward(d).wait_send()

    store.wait()


def on_device(
    sizes,
    offsets,
    anchor,
    stiffness,
    lattice_block,
    tile_ids,
    populations,
    visc_class,
    fluid_mask,
    tau_table,
):
    groups = sizes[1] * sizes[2]
    verts = offsets.shape[1]
    vmem = pl.BlockSpec(memory_space=pltpu.VMEM)
    smem = pl.BlockSpec(memory_space=pltpu.SMEM)
    hbm = pl.BlockSpec(memory_space=pl.ANY)
    return pl.pallas_call(
        functools.partial(kernel, sizes),
        out_shape=(
            jax.ShapeDtypeStruct(populations.shape, F32),
            jax.ShapeDtypeStruct((3, verts), F32),
        ),
        in_specs=[vmem] * 5 + [smem] + [hbm] * 3,
        out_specs=(hbm, vmem),
        scratch_shapes=[
            pltpu.VMEM((19, BX, BY, BZ), F32),
            pltpu.VMEM((BX, BY, BZ), I32),
            pltpu.VMEM((BX, BY, BZ), I32),
            pltpu.VMEM((16, verts), F32),
            pltpu.VMEM((CAP, verts), BF16),
            pltpu.VMEM((groups * 16, verts), BF16),
            pltpu.VMEM((groups, 8, CAP), F32),
            pltpu.VMEM((groups, 8, CAP), F32),
            pltpu.VMEM((2 * BZ, groups * CAP), BF16),
            pltpu.VMEM((SITES, groups * CAP), F32),
            pltpu.VMEM((6 * SITES, groups * CAP), BF16),
            pltpu.VMEM((6 * SITES, 2 * BZ), F32),
            pltpu.VMEM((3 * SITES, BZ), F32),
            pltpu.VMEM((2, 19 * XPAD * YPAD, BZ), F32),
            pltpu.VMEM((2, 2, 5, BY, BZ), F32),
            pltpu.VMEM((2, 2, 5, BY, BZ), F32),
            pltpu.VMEM((2, 2, 5, BX, BZ), F32),
            pltpu.VMEM((2, 2, 5, BX, BZ), F32),
            pltpu.VMEM((2, 2, 2, BX, BZ), F32),
            pltpu.VMEM((2, 2, BY, 128), F32),
            pltpu.VMEM((2, 2, BY, 128), F32),
            pltpu.VMEM((2, 2, 2, BY, 128), F32),
            pltpu.VMEM((2, 2, 2, 8, 128), F32),
            pltpu.VMEM((2, 2, YPAD, 128), F32),
            pltpu.VMEM((3 * SITES, BZ), F32),
            pltpu.VMEM((19, BX, BY, BZ), F32),
            pltpu.VMEM((groups * 8, CAP), F32),
            pltpu.VMEM((groups * 8, CAP), F32),
            pltpu.SemaphoreType.DMA((3,)),
            pltpu.SemaphoreType.DMA,
            pltpu.SemaphoreType.DMA((groups,)),
            pltpu.SemaphoreType.DMA((groups,)),
            pltpu.SemaphoreType.DMA((2, 18)),
            pltpu.SemaphoreType.DMA((2, 18)),
            pltpu.SemaphoreType.DMA((groups,)),
            pltpu.SemaphoreType.DMA((groups,)),
        ],
        compiler_params=pltpu.CompilerParams(
            collective_id=0, has_side_effects=True, vmem_limit_bytes=48 * 1024 * 1024
        ),
    )(
        offsets,
        anchor,
        stiffness.reshape(1, verts),
        lattice_block.reshape(1, verts),
        tile_ids.reshape(1, verts),
        tau_table,
        populations,
        visc_class,
        fluid_mask,
    )


def solution(mesh):
    placed = (
        P(None, ("gx", "gy", "gz")),
        P(None, ("gx", "gy", "gz")),
        P(("gx", "gy", "gz")),
        P(("gx", "gy", "gz"), None),
        P(("gx", "gy", "gz")),
        P(None, "gx", "gy", "gz"),
        P("gx", "gy", "gz"),
        P("gx", "gy", "gz"),
        P(),
    )
    sizes = tuple(mesh.shape[axis] for axis in ("gx", "gy", "gz"))
    return jax.shard_map(
        functools.partial(on_device, sizes),
        mesh=mesh,
        in_specs=placed,
        out_specs=(P(None, "gx", "gy", "gz"), P(None, ("gx", "gy", "gz"))),
        check_vma=False,
    )
```

```python
import functools

import jax
import jax.numpy as jnp
from jax import lax
from jax.experimental import pallas as pl
from jax.experimental.pallas import tpu as pltpu
from jax.sharding import PartitionSpec as P

MESH = pl.DeviceIdType.MESH
CAP = 128
BX, BY, BZ = 8, 16, 128
SITES = BX * BY
TZ = 32
WIDE = 4
PIECES = [pl.ds(start, min(5, 19 - start)) for start in range(0, 19, 5)]
PARTS = (8, 8, 8, 4, 4)
XPAD, YPAD = BX + 2, 32
F32, BF16, I32 = jnp.float32, jnp.bfloat16, jnp.int32

lattice_velocity = [
    (0, 0, 0),
    (1, 0, 0),
    (-1, 0, 0),
    (0, 1, 0),
    (0, -1, 0),
    (0, 0, 1),
    (0, 0, -1),
    (1, 1, 0),
    (-1, -1, 0),
    (1, -1, 0),
    (-1, 1, 0),
    (1, 0, 1),
    (-1, 0, -1),
    (1, 0, -1),
    (-1, 0, 1),
    (0, 1, 1),
    (0, -1, -1),
    (0, 1, -1),
    (0, -1, 1),
]
lattice_weight = [1.0 / 3.0] + [1.0 / 18.0] * 6 + [1.0 / 36.0] * 12
speed_scale = 20.0
pairs = [(i, i + 1) for i in range(1, 19, 2)]


def crossing(axis, sign):
    return [i for i in range(19) if lattice_velocity[i][axis] == sign]


XSET = [crossing(0, 1), crossing(0, -1)]
YSET = [crossing(1, 1), crossing(1, -1)]
ZSET = [crossing(2, 1), crossing(2, -1)]


def dist_of(*velocity):
    return lattice_velocity.index(tuple(velocity))


def z_lane(side, index, x):
    return ZSET[side].index(index) * XPAD + x + 1


def row_of(index, x, y):
    return (index * XPAD + x + 1) * YPAD + 8 + y


def moments(f, force):
    density = functools.reduce(lambda a, b: a + b, f)
    inverse = 1.0 / density
    flow = []
    for axis in range(3):
        plus = [f[i] for i in crossing(axis, 1)]
        minus = [f[i] for i in crossing(axis, -1)]
        total = functools.reduce(lambda a, b: a + b, plus) - functools.reduce(lambda a, b: a + b, minus)
        flow.append((total + 0.5 * force[axis]) * inverse)
    return density, flow


def collide(f, force, omega, fluid):
    density, flow = moments(f, force)
    speed_sq = flow[0] * flow[0] + flow[1] * flow[1] + flow[2] * flow[2]
    work = flow[0] * force[0] + flow[1] * force[1] + flow[2] * force[2]
    gain = 1.0 - 0.5 * omega
    keep = 1.0 - omega
    amount = omega * density
    base = amount * (1.0 - 1.5 * speed_sq) - (3.0 * gain) * work
    momentum = [amount * flow[a] for a in range(3)]
    push = [gain * force[a] for a in range(3)]
    steep = [4.5 * momentum[a] + 9.0 * push[a] for a in range(3)]
    slope = [3.0 * (momentum[a] + push[a]) for a in range(3)]
    result = [None] * 19
    result[0] = jnp.where(fluid, keep * f[0] + lattice_weight[0] * base, f[0])

    def along(values, velocity):
        total = None
        for axis in range(3):
            if velocity[axis]:
                if total is None:
                    total = values[axis] if velocity[axis] > 0 else -values[axis]
                else:
                    total = total + values[axis] if velocity[axis] > 0 else total - values[axis]
        return total

    for i, j in pairs:
        velocity = lattice_velocity[i]
        even = base + along(flow, velocity) * along(steep, velocity)
        odd = along(slope, velocity)
        weight = lattice_weight[i]
        result[i] = jnp.where(fluid, keep * f[i] + weight * (even + odd), f[j])
        result[j] = jnp.where(fluid, keep * f[j] + weight * (even - odd), f[i])
    return result


def kernel(
    sizes,
    off_hbm,
    anc_hbm,
    stf_hbm,
    tgt_hbm,
    tid_hbm,
    tau_hbm,
    pop_hbm,
    cls_hbm,
    flu_hbm,
    out_hbm,
    vel_ref,
    off_ref,
    anc_ref,
    stf_ref,
    tgt_ref,
    tid_ref,
    tau_ref,
    pops,
    cls,
    flu,
    rows,
    rt,
    lhs,
    outbuf,
    inbuf,
    wz,
    wxy,
    load,
    acc,
    force,
    field0,
    field1,
    xs,
    xr,
    ys,
    yr,
    xyr,
    zs,
    ze,
    zr,
    xzr,
    yzr,
    zp,
    ubuf,
    newp,
    vbuf,
    ret,
    in_sem,
    out_sem,
    fwd_send,
    fwd_recv,
    halo_send,
    halo_recv,
    back_send,
    back_recv,
):
    n_gx, n_gy, n_gz = sizes
    field = (field0, field1)
    groups = n_gy * n_gz
    verts = off_ref.shape[1]
    chunks = verts // 128
    gx, gy, gz = lax.axis_index("gx"), lax.axis_index("gy"), lax.axis_index("gz")

    def device(dx, dy, dz):
        return (
            lax.rem(gx + dx + n_gx, n_gx),
            lax.rem(gy + dy + n_gy, n_gy),
            lax.rem(gz + dz + n_gz, n_gz),
        )

    arguments = [
        (tgt_hbm, tgt_ref),
        (off_hbm, off_ref),
        (anc_hbm, anc_ref),
        (stf_hbm, stf_ref),
        (tid_hbm, tid_ref),
        (tau_hbm, tau_ref),
        (cls_hbm, cls),
        (flu_hbm, flu),
        (pop_hbm, pops),
    ]
    ring = sorted(
        ((dy, dz) for dy in range(n_gy) for dz in range(n_gz)),
        key=lambda at: (min(at[0], n_gy - at[0]) + min(at[1], n_gz - at[1]), at),
    )
    loads = [pltpu.make_async_copy(src, dst, in_sem.at[k]) for k, (src, dst) in enumerate(arguments)]
    for copy in loads:
        copy.start()

    barrier = pltpu.get_barrier_semaphore()

    @pl.loop(1, groups)
    def _(d):
        pl.semaphore_signal(
            barrier, inc=1, device_id=device(0, d // n_gz, lax.rem(d, n_gz)), device_id_type=MESH
        )

    others = [(sx, 0, 0) for sx in (1, -1)]
    others += [(sx, sy, 0) for sx in (1, -1) for sy in (1, -1)]
    others += [(sx, 0, sz) for sx in (1, -1) for sz in (1, -1)]
    for offset in others:
        pl.semaphore_signal(barrier, inc=1, device_id=device(*offset), device_id_type=MESH)

    loads[0].wait()
    target = tgt_ref[...]
    rel_y = lax.rem(target // n_gz - gy + n_gy, n_gy)
    rel_z = lax.rem(lax.rem(target, n_gz) - gz + n_gz, n_gz)
    rel = rel_y * n_gz + rel_z
    member = rel == lax.broadcasted_iota(I32, (groups, verts), 0)
    member_f = jnp.where(member, 1.0, 0.0).astype(F32)
    stacked = jnp.concatenate([member_f[:, c * 128 : (c + 1) * 128] for c in range(chunks)], axis=0)
    row_id = lax.broadcasted_iota(I32, (128, 256), 0)
    col_id = lax.broadcasted_iota(I32, (128, 256), 1)
    prefix = jnp.where((row_id < col_id) | (col_id >= 128), 1.0, 0.0).astype(BF16)
    counts = jnp.dot(stacked.astype(BF16), prefix, preferred_element_type=F32)
    base = jnp.zeros((groups, 128), F32)
    slot_id = lax.broadcasted_iota(I32, (128, 128), 0).astype(F32)
    for c in range(chunks):
        part = counts[c * groups : (c + 1) * groups]
        rank = jnp.sum(
            member_f[:, c * 128 : (c + 1) * 128] * (part[:, :128] + base), axis=0, keepdims=True
        )
        base = base + part[:, 128:]
        rt[:, c * 128 : (c + 1) * 128] = jnp.where(rank == slot_id, 1.0, 0.0).astype(BF16)

    def high(value):
        return value.astype(BF16).astype(F32)

    for copy in loads[1:5]:
        copy.wait()
    offs = off_ref[...]
    push = stf_ref[...] * (anc_ref[...] - offs)
    offs_hi = high(offs)
    offs_mid = high(offs - offs_hi)
    push_hi = high(push)
    rows[...] = jnp.zeros((16, verts), F32)
    rows[0:3, :] = offs_hi
    rows[3:6, :] = push_hi
    rows[6:7, :] = tid_ref[...].astype(F32)
    rows[7:8, :] = (offs - offs_hi - offs_mid)[2:3]
    rows[8:11, :] = offs_mid
    rows[11:14, :] = push - push_hi
    for d in range(groups):
        lhs[d * 16 : (d + 1) * 16, :] = jnp.where(rel == d, rows[...], 0.0).astype(BF16)
    packed = lax.dot_general(
        lhs[...], rt[...], (((1,), (1,)), ((), ())), preferred_element_type=F32
    )
    sub8 = lax.broadcasted_iota(I32, (8, 128), 0)
    lane8 = lax.broadcasted_iota(I32, (8, 128), 1)
    for d in range(groups):
        both = packed[d * 16 : d * 16 + 8] + packed[d * 16 + 8 : d * 16 + 16]
        fine = pltpu.roll(both, 3, axis=0)
        outbuf[d] = both + jnp.where(sub8 == 2, fine, 0.0)
    inbuf[0] = outbuf[0]

    pl.semaphore_wait(barrier, groups - 1 + len(others))

    def forward(k, dy=0, dz=1):
        return pltpu.make_async_remote_copy(
            src_ref=outbuf.at[dy * n_gz + dz],
            dst_ref=inbuf.at[k],
            send_sem=fwd_send.at[k],
            recv_sem=fwd_recv.at[k],
            device_id=device(0, dy, dz),
            device_id_type=MESH,
        )

    for k in range(groups - 1, 0, -1):
        forward(k, *ring[k]).start()

    wide = 128 * WIDE
    x_id = lax.broadcasted_iota(I32, (BX, wide), 0)
    y_id = lax.broadcasted_iota(I32, (BY, wide), 0)
    z_half = 0.5 * lax.broadcasted_iota(I32, (TZ, wide), 0).astype(F32)
    third = 1.0 / 1.5

    def split(value):
        top = value.astype(BF16)
        return top, (value - top.astype(F32)).astype(BF16)

    def spread(at):
        blk = jnp.concatenate([inbuf[at * WIDE + e] for e in range(WIDE)], axis=1)
        tile = blk[6:7].astype(I32)
        tile_x, tile_y, tile_z = tile // 32, lax.rem(tile // 4, 8), lax.rem(tile, 4)
        dist_x = 2.0 * blk[0:1] - lax.rem(x_id, 2).astype(F32)
        wx = jnp.where(x_id // 2 == tile_x, jnp.maximum(0.0, 1.0 - jnp.abs(dist_x) * third), 0.0)
        dist_y = 2.0 * blk[1:2] - lax.rem(y_id, 2).astype(F32)
        wy = jnp.where(y_id // 2 == tile_y, jnp.maximum(0.0, 1.0 - jnp.abs(dist_y) * third), 0.0)
        weight = jnp.maximum(0.0, 1.0 - jnp.abs(16.0 * blk[2:3] - z_half))
        lanes = pl.ds(pl.multiple_of(at * wide, wide), wide)
        wz[:, lanes] = weight
        for x in range(BX):
            for part, value in enumerate(split(wx[x : x + 1] * wy)):
                row = part * SITES + x * BY
                wxy[row : row + BY, lanes] = value
        for c in range(3):
            for part, value in enumerate(split(weight * blk[3 + c : 4 + c])):
                for z in range(BZ // TZ):
                    row = (part * 3 + c) * BZ + z * TZ
                    load[row : row + TZ, lanes] = jnp.where(
                        jnp.broadcast_to(tile_z == z, (TZ, wide)), value, jnp.zeros_like(value)
                    )

    first_slot = 0
    for count in PARTS:

        @pl.loop(max(first_slot, 1), first_slot + count)
        def _(k):
            forward(k).wait_recv()

        @pl.loop(first_slot // WIDE, (first_slot + count) // WIDE)
        def _(at):
            spread(at)

        span = slice(first_slot * 128, (first_slot + count) * 128)
        product = lax.dot_general(
            wxy[:, span], load[:, span], (((1,), (1,)), ((), ())), preferred_element_type=F32
        )
        if first_slot == 0:
            acc[...] = product
        else:
            acc[...] += product
        first_slot += count
    for c in range(3):
        here, there = slice(c * BZ, (c + 1) * BZ), slice((3 + c) * BZ, (4 + c) * BZ)
        force[c * SITES : (c + 1) * SITES, :] = (acc[0:SITES, here] + acc[0:SITES, there]) + (
            acc[SITES:, here] + acc[SITES:, there]
        )

    for copy in loads[5:]:
        copy.wait()

    taus = [1.0 / jnp.full((8, 128), tau_ref[k], F32) for k in range(4)]

    def site_values(x, h):
        rows_at = slice(8 * h, 8 * h + 8)
        klass = cls[x, rows_at, :]
        omega = jnp.where(
            klass < 2, jnp.where(klass == 0, taus[0], taus[1]), jnp.where(klass == 2, taus[2], taus[3])
        )
        return omega, flu[x, rows_at, :] > 0

    def forces(x, h):
        starts = [c * SITES + x * BY + 8 * h for c in range(3)]
        return [force[start : start + 8, :] for start in starts]

    def messages(p):
        early, late = [], []
        for s, sign in enumerate((1, -1)):
            early.append(((sign, 0, 0), xs.at[p, s], xr.at[p, s]))
            late.append(((0, sign, 0), ys.at[p, s], yr.at[p, s]))
            late.append(((0, 0, sign), zs.at[p, s], zr.at[p, s]))
            for t, other in enumerate((1, -1)):
                edge = pl.ds(8 if other > 0 else 0, 8)
                spot = XSET[s].index(dist_of(sign, other, 0))
                early.append(((sign, other, 0), xs.at[p, s, spot, edge], xyr.at[p, s, t]))
                early.append(((other, 0, sign), ze.at[p, s], xzr.at[p, s, t]))
                late.append(((0, other, sign), zs.at[p, s, edge], yzr.at[p, s, t]))
        hops = lambda message: -sum(abs(v) for v in message[0])
        return sorted(early, key=hops), sorted(late, key=hops)

    def halo(p):
        early, late = messages(p)
        return [
            pltpu.make_async_remote_copy(
                src_ref=src,
                dst_ref=dst,
                send_sem=halo_send.at[p, m],
                recv_sem=halo_recv.at[p, m],
                device_id=device(*offset),
                device_id_type=MESH,
            )
            for m, (offset, src, dst) in enumerate(early + late)
        ], len(early)

    def streamed(p, x, h):
        found = []
        for i in range(19):
            cx, cy, cz = lattice_velocity[i]
            start = row_of(i, x - cx, 8 * h - cy)
            value = field[p][start : start + 8, :]
            if cz:
                s = 0 if cz > 0 else 1
                border = zp[p, s, 8 + 8 * h - cy : 16 + 8 * h - cy, :]
                lane = z_lane(s, i, x - cx)
                edge = 0 if cz > 0 else 127
                shift = 128 - lane if cz > 0 else 127 - lane
                value = jnp.where(
                    lane8 == edge,
                    pltpu.roll(border, shift, axis=1),
                    pltpu.roll(value, 1 if cz > 0 else 127, axis=1),
                )
            found.append(value)
        return found

    def sweep(p, source, earlier):
        def plane(x, borders):
            incoming = [source(x, h) for h in range(2)]
            for h in range(2):
                omega, fluid = site_values(x, h)
                result = collide(incoming[h], forces(x, h), omega, fluid)
                for i in range(19):
                    start = row_of(i, x, 8 * h)
                    field[p][start : start + 8, :] = result[i]
                for s in range(2):
                    for i in ZSET[s]:
                        lane = z_lane(s, i, x)
                        shift = lane + 1 if s == 0 else lane
                        borders[2 * s + h] = jnp.where(
                            lane8 == lane, pltpu.roll(result[i], shift, axis=1), borders[2 * s + h]
                        )

        copies, early = halo(p)
        borders = [jnp.zeros((8, 128), F32)] * 4
        for x in (0, BX - 1):
            plane(x, borders)
        for s in range(2):
            for h in range(2):
                ze[p, s, 8 * h : 8 * h + 8, :] = borders[2 * s + h]
            for k, i in enumerate(XSET[s]):
                start = row_of(i, BX - 1 if s == 0 else 0, 0)
                xs[p, s, k] = field[p][start : start + BY, :]
        for copy in copies[:early]:
            copy.start()
        for x in range(1, BX - 1):
            plane(x, borders)
        for s in range(2):
            for h in range(2):
                zs[p, s, 8 * h : 8 * h + 8, :] = borders[2 * s + h]
            for k, i in enumerate(YSET[s]):
                ys[p, s, k] = field[p][pl.ds(row_of(i, 0, BY - 1 if s == 0 else 0), BX, stride=YPAD), :]
        for copy in copies[early:]:
            copy.start()
        earlier()
        for copy in copies:
            copy.wait_recv()
        lane16 = lax.broadcasted_iota(I32, (BY, 128), 1)
        for s, sign in enumerate((1, -1)):
            for k, i in enumerate(XSET[s]):
                start = row_of(i, -1 if s == 0 else BX, 0)
                field[p][start : start + BY, :] = xr[p, s, k]
            for k, i in enumerate(YSET[s]):
                field[p][pl.ds(row_of(i, 0, -1 if s == 0 else BY), BX, stride=YPAD), :] = yr[p, s, k]
            plane = zr[p, s]
            for t, other in enumerate((1, -1)):
                to, row = (-1, 7) if other > 0 else (BY, 0)
                start = row_of(dist_of(sign, other, 0), -1 if s == 0 else BX, to)
                field[p][start : start + 1, :] = xyr[p, s, t, row : row + 1, :]
                zp[p, s, 8 + to : 9 + to, :] = yzr[p, s, t, row : row + 1, :]
                i = dist_of(other, 0, sign)
                lane = z_lane(s, i, -1 if other > 0 else BX)
                shift = 128 - BX if other > 0 else BX
                plane = jnp.where(lane16 == lane, pltpu.roll(xzr[p, s, t], shift, axis=1), plane)
            zp[p, s, 8:24, :] = plane
        return copies

    def first(x, h):
        return [pops[i, x, 8 * h : 8 * h + 8, :] for i in range(19)]

    def forward_sent():
        @pl.loop(1, groups)
        def _(k):
            forward(k).wait_send()

    def halo_sent(copies):
        for copy in copies:
            copy.wait_send()

    sent = sweep(0, first, forward_sent)
    sent = sweep(1, functools.partial(streamed, 0), functools.partial(halo_sent, sent))

    for x in range(BX):
        incoming = [streamed(1, x, h) for h in range(2)]
        for h in range(2):
            for i in range(19):
                newp[i, x, 8 * h : 8 * h + 8, :] = incoming[h][i]
            density, flow = moments(incoming[h], forces(x, h))
            for c in range(3):
                start = c * SITES + x * BY + 8 * h
                ubuf[start : start + 8, :] = flow[c]

    store = pltpu.make_async_copy(newp, out_hbm, out_sem)
    store.start()

    turned = [[], []]
    for c in range(3):
        for part, value in enumerate(split(ubuf[c * SITES : (c + 1) * SITES, :].T)):
            turned[part].append(value)
    flow_hi, flow_lo = (jnp.concatenate(part, axis=0) for part in turned)
    flow_all = jnp.concatenate([flow_hi, flow_hi, flow_lo, flow_lo], axis=1)

    def backward(k, dy=0, dz=1):
        return pltpu.make_async_remote_copy(
            src_ref=vbuf.at[k],
            dst_ref=ret.at[dy * n_gz + dz],
            send_sem=back_send.at[k],
            recv_sem=back_recv.at[k],
            device_id=device(0, -dy, -dz),
            device_id_type=MESH,
        )

    for pair in range(groups // 2 - 1, -1, -1):
        lanes = slice(pair * 256, (pair + 1) * 256)
        block = wxy[:, lanes]
        picked = jnp.dot(
            flow_all, jnp.concatenate([block, block], axis=0), preferred_element_type=F32
        )
        weight = wz[:, lanes]
        tile = jnp.concatenate([inbuf[2 * pair + e, 6:7, :] for e in range(2)], axis=1)
        tile_z = jnp.broadcast_to(lax.rem(tile.astype(I32), 4), (TZ, 256))
        for c in range(3):
            speed = picked[c * BZ : c * BZ + TZ]
            for z in range(1, BZ // TZ):
                at = c * BZ + z * TZ
                speed = jnp.where(tile_z == z, picked[at : at + TZ], speed)
            speed = speed_scale * jnp.sum(speed * weight, axis=0, keepdims=True)
            for e in range(2):
                vbuf[2 * pair + e, c : c + 1, :] = speed[:, e * 128 : (e + 1) * 128]
        for k in (2 * pair + 1, 2 * pair):
            if k > 0:
                backward(k, *ring[k]).start()

    halo_sent(sent)
    ret[0] = vbuf[0]

    @pl.loop(1, groups)
    def _(k):
        backward(k).wait_recv()

    answer = jnp.concatenate([ret[:, c, :] for c in range(3)], axis=0)
    answer_hi = answer.astype(BF16)
    answer_lo = (answer - answer_hi.astype(F32)).astype(BF16)
    found = jnp.dot(
        jnp.concatenate([answer_hi, answer_lo], axis=0), rt[...], preferred_element_type=F32
    )
    found = found[0 : 3 * groups] + found[3 * groups :]
    for c in range(3):
        vel_ref[c : c + 1, :] = jnp.sum(
            jnp.where(member, found[c * groups : (c + 1) * groups], 0.0), axis=0, keepdims=True
        )

    @pl.loop(1, groups)
    def _(k):
        backward(k).wait_send()

    store.wait()


def hand_over(new_hbm, vel_hbm, new_out, vel_out, new_ref, vel_ref, sems):
    hops = [(vel_hbm, vel_ref, vel_out)]
    hops += [(new_hbm.at[part], new_ref.at[part], new_out.at[part]) for part in PIECES]
    inward = [pltpu.make_async_copy(src, mid, sems.at[0, k]) for k, (src, mid, _) in enumerate(hops)]
    outward = [pltpu.make_async_copy(mid, dst, sems.at[1, k]) for k, (_, mid, dst) in enumerate(hops)]
    for copy in inward:
        copy.start()
    for k, copy in enumerate(inward):
        copy.wait()
        outward[k].start()
    for copy in outward:
        copy.wait()


def on_device(
    sizes,
    offsets,
    anchor,
    stiffness,
    lattice_block,
    tile_ids,
    populations,
    visc_class,
    fluid_mask,
    tau_table,
):
    groups = sizes[1] * sizes[2]
    verts = offsets.shape[1]
    vmem = pl.BlockSpec(memory_space=pltpu.VMEM)
    hbm = pl.BlockSpec(memory_space=pltpu.HBM)
    results = pl.pallas_call(
        functools.partial(kernel, sizes),
        out_shape=(
            jax.ShapeDtypeStruct(populations.shape, F32),
            jax.ShapeDtypeStruct((3, verts), F32),
        ),
        in_specs=[hbm] * 9,
        out_specs=(hbm, vmem),
        scratch_shapes=[
            pltpu.VMEM((3, verts), F32),
            pltpu.VMEM((3, verts), F32),
            pltpu.VMEM((1, verts), F32),
            pltpu.VMEM((1, verts), I32),
            pltpu.VMEM((1, verts), I32),
            pltpu.SMEM((4,), F32),
            pltpu.VMEM((19, BX, BY, BZ), F32),
            pltpu.VMEM((BX, BY, BZ), I32),
            pltpu.VMEM((BX, BY, BZ), I32),
            pltpu.VMEM((16, verts), F32),
            pltpu.VMEM((CAP, verts), BF16),
            pltpu.VMEM((groups * 16, verts), BF16),
            pltpu.VMEM((groups, 8, CAP), F32),
            pltpu.VMEM((groups, 8, CAP), F32),
            pltpu.VMEM((TZ, groups * CAP), F32),
            pltpu.VMEM((2 * SITES, groups * CAP), BF16),
            pltpu.VMEM((6 * BZ, groups * CAP), BF16),
            pltpu.VMEM((2 * SITES, 6 * BZ), F32),
            pltpu.VMEM((3 * SITES, BZ), F32),
            pltpu.VMEM((19 * XPAD * YPAD, BZ), F32),
            pltpu.VMEM((19 * XPAD * YPAD, BZ), F32),
            pltpu.VMEM((2, 2, 5, BY, BZ), F32),
            pltpu.VMEM((2, 2, 5, BY, BZ), F32),
            pltpu.VMEM((2, 2, 5, BX, BZ), F32),
            pltpu.VMEM((2, 2, 5, BX, BZ), F32),
            pltpu.VMEM((2, 2, 2, BX, BZ), F32),
            pltpu.VMEM((2, 2, BY, 128), F32),
            pltpu.VMEM((2, 2, BY, 128), F32),
            pltpu.VMEM((2, 2, BY, 128), F32),
            pltpu.VMEM((2, 2, 2, BY, 128), F32),
            pltpu.VMEM((2, 2, 2, 8, 128), F32),
            pltpu.VMEM((2, 2, YPAD, 128), F32),
            pltpu.VMEM((3 * SITES, BZ), F32),
            pltpu.VMEM((19, BX, BY, BZ), F32),
            pltpu.VMEM((groups, 4, CAP), F32),
            pltpu.VMEM((groups, 4, CAP), F32),
            pltpu.SemaphoreType.DMA((9,)),
            pltpu.SemaphoreType.DMA,
            pltpu.SemaphoreType.DMA((groups,)),
            pltpu.SemaphoreType.DMA((groups,)),
            pltpu.SemaphoreType.DMA((2, 18)),
            pltpu.SemaphoreType.DMA((2, 18)),
            pltpu.SemaphoreType.DMA((groups,)),
            pltpu.SemaphoreType.DMA((groups,)),
        ],
        compiler_params=pltpu.CompilerParams(
            collective_id=0, has_side_effects=True, vmem_limit_bytes=60 * 1024 * 1024
        ),
    )(
        offsets,
        anchor,
        stiffness.reshape(1, verts),
        lattice_block.reshape(1, verts),
        tile_ids.reshape(1, verts),
        tau_table,
        populations,
        visc_class,
        fluid_mask,
    )
    return pl.pallas_call(
        hand_over,
        out_shape=[jax.ShapeDtypeStruct(result.shape, F32) for result in results],
        in_specs=[hbm] * 2,
        out_specs=[hbm] * 2,
        scratch_shapes=[
            pltpu.VMEM(populations.shape, F32),
            pltpu.VMEM((3, verts), F32),
            pltpu.SemaphoreType.DMA((2, 1 + len(PIECES))),
        ],
        compiler_params=pltpu.CompilerParams(vmem_limit_bytes=60 * 1024 * 1024),
    )(*results)


def solution(mesh):
    placed = (
        P(None, ("gx", "gy", "gz")),
        P(None, ("gx", "gy", "gz")),
        P(("gx", "gy", "gz")),
        P(("gx", "gy", "gz"), None),
        P(("gx", "gy", "gz")),
        P(None, "gx", "gy", "gz"),
        P("gx", "gy", "gz"),
        P("gx", "gy", "gz"),
        P(),
    )
    sizes = tuple(mesh.shape[axis] for axis in ("gx", "gy", "gz"))
    return jax.shard_map(
        functools.partial(on_device, sizes),
        mesh=mesh,
        in_specs=placed,
        out_specs=(P(None, "gx", "gy", "gz"), P(None, ("gx", "gy", "gz"))),
        check_vma=False,
    )
```

```python
import functools

import jax
import jax.numpy as jnp
from jax import lax
from jax.experimental import pallas as pl
from jax.experimental.pallas import tpu as pltpu
from jax.sharding import PartitionSpec as P

MESH = pl.DeviceIdType.MESH
CAP = 128
BX, BY, BZ = 8, 16, 128
SITES = BX * BY
TZ = 32
WIDE = 4
PIECES = [pl.ds(start, min(5, 19 - start)) for start in range(0, 19, 5)]
PART = 8
XPAD, YPAD = BX + 2, 32
F32, BF16, I32 = jnp.float32, jnp.bfloat16, jnp.int32

lattice_velocity = [
    (0, 0, 0),
    (1, 0, 0),
    (-1, 0, 0),
    (0, 1, 0),
    (0, -1, 0),
    (0, 0, 1),
    (0, 0, -1),
    (1, 1, 0),
    (-1, -1, 0),
    (1, -1, 0),
    (-1, 1, 0),
    (1, 0, 1),
    (-1, 0, -1),
    (1, 0, -1),
    (-1, 0, 1),
    (0, 1, 1),
    (0, -1, -1),
    (0, 1, -1),
    (0, -1, 1),
]
lattice_weight = [1.0 / 3.0] + [1.0 / 18.0] * 6 + [1.0 / 36.0] * 12
speed_scale = 20.0
pairs = [(i, i + 1) for i in range(1, 19, 2)]


def crossing(axis, sign):
    return [i for i in range(19) if lattice_velocity[i][axis] == sign]


XSET = [crossing(0, 1), crossing(0, -1)]
YSET = [crossing(1, 1), crossing(1, -1)]
ZSET = [crossing(2, 1), crossing(2, -1)]


def dist_of(*velocity):
    return lattice_velocity.index(tuple(velocity))


def z_lane(side, index, x):
    return ZSET[side].index(index) * XPAD + x + 1


def row_of(index, x, y):
    return (index * XPAD + x + 1) * YPAD + 8 + y


def moments(f, force):
    density = functools.reduce(lambda a, b: a + b, f)
    inverse = 1.0 / density
    flow = []
    for axis in range(3):
        plus = [f[i] for i in crossing(axis, 1)]
        minus = [f[i] for i in crossing(axis, -1)]
        total = functools.reduce(lambda a, b: a + b, plus) - functools.reduce(lambda a, b: a + b, minus)
        flow.append((total + 0.5 * force[axis]) * inverse)
    return density, flow


def collide(f, force, omega, fluid):
    density, flow = moments(f, force)
    speed_sq = flow[0] * flow[0] + flow[1] * flow[1] + flow[2] * flow[2]
    work = flow[0] * force[0] + flow[1] * force[1] + flow[2] * force[2]
    gain = 1.0 - 0.5 * omega
    keep = 1.0 - omega
    amount = omega * density
    base = amount * (1.0 - 1.5 * speed_sq) - (3.0 * gain) * work
    momentum = [amount * flow[a] for a in range(3)]
    push = [gain * force[a] for a in range(3)]
    steep = [4.5 * momentum[a] + 9.0 * push[a] for a in range(3)]
    slope = [3.0 * (momentum[a] + push[a]) for a in range(3)]
    result = [None] * 19
    result[0] = jnp.where(fluid, keep * f[0] + lattice_weight[0] * base, f[0])

    def along(values, velocity):
        total = None
        for axis in range(3):
            if velocity[axis]:
                if total is None:
                    total = values[axis] if velocity[axis] > 0 else -values[axis]
                else:
                    total = total + values[axis] if velocity[axis] > 0 else total - values[axis]
        return total

    for i, j in pairs:
        velocity = lattice_velocity[i]
        even = base + along(flow, velocity) * along(steep, velocity)
        odd = along(slope, velocity)
        weight = lattice_weight[i]
        result[i] = jnp.where(fluid, keep * f[i] + weight * (even + odd), f[j])
        result[j] = jnp.where(fluid, keep * f[j] + weight * (even - odd), f[i])
    return result


def kernel(
    sizes,
    off_hbm,
    anc_hbm,
    stf_hbm,
    tgt_hbm,
    tid_hbm,
    tau_hbm,
    pop_hbm,
    cls_hbm,
    flu_hbm,
    out_hbm,
    ret_hbm,
    rank_hbm,
    rel_hbm,
    off_ref,
    anc_ref,
    stf_ref,
    tgt_ref,
    tid_ref,
    tau_ref,
    pops,
    cls,
    flu,
    rank_ref,
    rel_ref,
    rows,
    rt,
    lhs,
    outbuf,
    inbuf,
    wz,
    wxy,
    load,
    acc,
    force,
    field0,
    field1,
    xs,
    xr,
    ys,
    yr,
    xyr,
    zs,
    ze,
    zr,
    xzr,
    yzr,
    zp,
    ubuf,
    newp,
    vbuf,
    in_sem,
    out_sem,
    fwd_send,
    fwd_recv,
    halo_send,
    halo_recv,
    back_send,
    back_recv,
):
    n_gx, n_gy, n_gz = sizes
    field = (field0, field1)
    groups = n_gy * n_gz
    verts = off_ref.shape[1]
    chunks = verts // 128
    gx, gy, gz = lax.axis_index("gx"), lax.axis_index("gy"), lax.axis_index("gz")

    def device(dx, dy, dz):
        return (
            lax.rem(gx + dx + n_gx, n_gx),
            lax.rem(gy + dy + n_gy, n_gy),
            lax.rem(gz + dz + n_gz, n_gz),
        )

    arguments = [
        (tgt_hbm, tgt_ref),
        (off_hbm, off_ref),
        (anc_hbm, anc_ref),
        (stf_hbm, stf_ref),
        (tid_hbm, tid_ref),
        (tau_hbm, tau_ref),
        (cls_hbm, cls),
        (flu_hbm, flu),
        (pop_hbm, pops),
    ]
    ring = sorted(
        ((dy, dz) for dy in range(n_gy) for dz in range(n_gz)),
        key=lambda at: (min(at[0], n_gy - at[0]) + min(at[1], n_gz - at[1]), at),
    )
    loads = [pltpu.make_async_copy(src, dst, in_sem.at[k]) for k, (src, dst) in enumerate(arguments)]
    barrier = pltpu.get_barrier_semaphore()

    for offset in ring[:0:-1]:
        pl.semaphore_signal(barrier, inc=1, device_id=device(0, *offset), device_id_type=MESH)
    others = [(sx, 0, 0) for sx in (1, -1)]
    others += [(sx, sy, 0) for sx in (1, -1) for sy in (1, -1)]
    others += [(sx, 0, sz) for sx in (1, -1) for sz in (1, -1)]
    for offset in others:
        pl.semaphore_signal(barrier, inc=1, device_id=device(*offset), device_id_type=MESH)

    for copy in loads:
        copy.start()

    loads[0].wait()
    target = tgt_ref[...]
    rel_y = lax.rem(target // n_gz - gy + n_gy, n_gy)
    rel_z = lax.rem(lax.rem(target, n_gz) - gz + n_gz, n_gz)
    rel = rel_y * n_gz + rel_z
    member = rel == lax.broadcasted_iota(I32, (groups, verts), 0)
    member_f = jnp.where(member, 1.0, 0.0).astype(F32)
    stacked = jnp.concatenate([member_f[:, c * 128 : (c + 1) * 128] for c in range(chunks)], axis=0)
    row_id = lax.broadcasted_iota(I32, (128, 256), 0)
    col_id = lax.broadcasted_iota(I32, (128, 256), 1)
    prefix = jnp.where((row_id < col_id) | (col_id >= 128), 1.0, 0.0).astype(BF16)
    counts = jnp.dot(stacked.astype(BF16), prefix, preferred_element_type=F32)
    base = jnp.zeros((groups, 128), F32)
    slot_id = lax.broadcasted_iota(I32, (128, 128), 0).astype(F32)
    for c in range(chunks):
        part = counts[c * groups : (c + 1) * groups]
        rank = jnp.sum(
            member_f[:, c * 128 : (c + 1) * 128] * (part[:, :128] + base), axis=0, keepdims=True
        )
        base = base + part[:, 128:]
        rt[:, c * 128 : (c + 1) * 128] = jnp.where(rank == slot_id, 1.0, 0.0).astype(BF16)
        rank_ref[:, c * 128 : (c + 1) * 128] = rank
    rel_ref[...] = rel
    kept = [
        pltpu.make_async_copy(rank_ref, rank_hbm, out_sem.at[1]),
        pltpu.make_async_copy(rel_ref, rel_hbm, out_sem.at[2]),
    ]
    for copy in kept:
        copy.start()

    def high(value):
        return value.astype(BF16).astype(F32)

    for copy in loads[1:5]:
        copy.wait()
    offs = off_ref[...]
    push = stf_ref[...] * (anc_ref[...] - offs)
    offs_hi = high(offs)
    offs_mid = high(offs - offs_hi)
    push_hi = high(push)
    rows[...] = jnp.zeros((16, verts), F32)
    rows[0:3, :] = offs_hi
    rows[3:6, :] = push_hi
    rows[6:7, :] = tid_ref[...].astype(F32)
    rows[7:8, :] = (offs - offs_hi - offs_mid)[2:3]
    rows[8:11, :] = offs_mid
    rows[11:14, :] = push - push_hi
    for d in range(groups):
        lhs[d * 16 : (d + 1) * 16, :] = jnp.where(rel == d, rows[...], 0.0).astype(BF16)
    packed = lax.dot_general(
        lhs[...], rt[...], (((1,), (1,)), ((), ())), preferred_element_type=F32
    )
    sub8 = lax.broadcasted_iota(I32, (8, 128), 0)
    lane8 = lax.broadcasted_iota(I32, (8, 128), 1)
    for d in range(groups):
        both = packed[d * 16 : d * 16 + 8] + packed[d * 16 + 8 : d * 16 + 16]
        fine = pltpu.roll(both, 3, axis=0)
        outbuf[d] = both + jnp.where(sub8 == 2, fine, 0.0)
    inbuf[0] = outbuf[0]

    pl.semaphore_wait(barrier, groups - 1 + len(others))

    def forward(k, dy=0, dz=1):
        return pltpu.make_async_remote_copy(
            src_ref=outbuf.at[dy * n_gz + dz],
            dst_ref=inbuf.at[k],
            send_sem=fwd_send.at[k],
            recv_sem=fwd_recv.at[k],
            device_id=device(0, dy, dz),
            device_id_type=MESH,
        )

    for k in range(1, groups):
        forward(k, *ring[k]).start()

    wide = 128 * WIDE
    x_id = lax.broadcasted_iota(I32, (BX, wide), 0)
    y_id = lax.broadcasted_iota(I32, (BY, wide), 0)
    z_half = 0.5 * lax.broadcasted_iota(I32, (TZ, wide), 0).astype(F32)
    third = 1.0 / 1.5

    def split(value):
        top = value.astype(BF16)
        return top, (value - top.astype(F32)).astype(BF16)

    def spread(part, at):
        first = part * PART + at * WIDE
        blk = jnp.concatenate([inbuf[first + e] for e in range(WIDE)], axis=1)
        tile = blk[6:7].astype(I32)
        tile_x, tile_y, tile_z = tile // 32, lax.rem(tile // 4, 8), lax.rem(tile, 4)
        dist_x = 2.0 * blk[0:1] - lax.rem(x_id, 2).astype(F32)
        wx = jnp.where(x_id // 2 == tile_x, jnp.maximum(0.0, 1.0 - jnp.abs(dist_x) * third), 0.0)
        dist_y = 2.0 * blk[1:2] - lax.rem(y_id, 2).astype(F32)
        wy = jnp.where(y_id // 2 == tile_y, jnp.maximum(0.0, 1.0 - jnp.abs(dist_y) * third), 0.0)
        weight = jnp.maximum(0.0, 1.0 - jnp.abs(16.0 * blk[2:3] - z_half))
        lanes = slice(at * wide, (at + 1) * wide)
        wz[part][:, lanes] = weight
        for x in range(BX):
            for piece, value in enumerate(split(wx[x : x + 1] * wy)):
                row = piece * SITES + x * BY
                wxy[part][row : row + BY, lanes] = value
        for c in range(3):
            for piece, value in enumerate(split(weight * blk[3 + c : 4 + c])):
                for z in range(BZ // TZ):
                    row = (piece * 3 + c) * BZ + z * TZ
                    load[part][row : row + TZ, lanes] = jnp.where(
                        jnp.broadcast_to(tile_z == z, (TZ, wide)), value, jnp.zeros_like(value)
                    )

    for part in range(groups // PART):
        for k in range(max(part * PART, 1), (part + 1) * PART):
            forward(k).wait_recv()
        for at in range(PART // WIDE):
            spread(part, at)
        product = lax.dot_general(
            wxy[part][...], load[part][...], (((1,), (1,)), ((), ())), preferred_element_type=F32
        )
        if part == 0:
            acc[...] = product
        else:
            acc[...] += product
    for c in range(3):
        here, there = slice(c * BZ, (c + 1) * BZ), slice((3 + c) * BZ, (4 + c) * BZ)
        force[c * SITES : (c + 1) * SITES, :] = (acc[0:SITES, here] + acc[0:SITES, there]) + (
            acc[SITES:, here] + acc[SITES:, there]
        )

    for copy in loads[5:]:
        copy.wait()

    taus = [1.0 / jnp.full((8, 128), tau_ref[k], F32) for k in range(4)]

    def site_values(x, h):
        rows_at = slice(8 * h, 8 * h + 8)
        klass = cls[x, rows_at, :]
        omega = jnp.where(
            klass < 2, jnp.where(klass == 0, taus[0], taus[1]), jnp.where(klass == 2, taus[2], taus[3])
        )
        return omega, flu[x, rows_at, :] > 0

    def forces(x, h):
        starts = [c * SITES + x * BY + 8 * h for c in range(3)]
        return [force[start : start + 8, :] for start in starts]

    def messages(p):
        early, late = [], []
        for s, sign in enumerate((1, -1)):
            early.append(((sign, 0, 0), xs.at[p, s], xr.at[p, s]))
            late.append(((0, sign, 0), ys.at[p, s], yr.at[p, s]))
            late.append(((0, 0, sign), zs.at[p, s], zr.at[p, s]))
            for t, other in enumerate((1, -1)):
                edge = pl.ds(8 if other > 0 else 0, 8)
                spot = XSET[s].index(dist_of(sign, other, 0))
                early.append(((sign, other, 0), xs.at[p, s, spot, edge], xyr.at[p, s, t]))
                early.append(((other, 0, sign), ze.at[p, s], xzr.at[p, s, t]))
                late.append(((0, other, sign), zs.at[p, s, edge], yzr.at[p, s, t]))
        hops = lambda message: -sum(abs(v) for v in message[0])
        return sorted(early, key=hops), sorted(late, key=hops)

    def halo(p):
        early, late = messages(p)
        return [
            pltpu.make_async_remote_copy(
                src_ref=src,
                dst_ref=dst,
                send_sem=halo_send.at[p, m],
                recv_sem=halo_recv.at[p, m],
                device_id=device(*offset),
                device_id_type=MESH,
            )
            for m, (offset, src, dst) in enumerate(early + late)
        ], len(early)

    def streamed(p, x, h):
        found = []
        for i in range(19):
            cx, cy, cz = lattice_velocity[i]
            start = row_of(i, x - cx, 8 * h - cy)
            value = field[p][start : start + 8, :]
            if cz:
                s = 0 if cz > 0 else 1
                border = zp[p, s, 8 + 8 * h - cy : 16 + 8 * h - cy, :]
                lane = z_lane(s, i, x - cx)
                edge = 0 if cz > 0 else 127
                shift = 128 - lane if cz > 0 else 127 - lane
                value = jnp.where(
                    lane8 == edge,
                    pltpu.roll(border, shift, axis=1),
                    pltpu.roll(value, 1 if cz > 0 else 127, axis=1),
                )
            found.append(value)
        return found

    def sweep(p, source, earlier):
        def plane(x, borders):
            incoming = [source(x, h) for h in range(2)]
            for h in range(2):
                omega, fluid = site_values(x, h)
                result = collide(incoming[h], forces(x, h), omega, fluid)
                for i in range(19):
                    start = row_of(i, x, 8 * h)
                    field[p][start : start + 8, :] = result[i]
                for s in range(2):
                    for i in ZSET[s]:
                        lane = z_lane(s, i, x)
                        shift = lane + 1 if s == 0 else lane
                        borders[2 * s + h] = jnp.where(
                            lane8 == lane, pltpu.roll(result[i], shift, axis=1), borders[2 * s + h]
                        )

        copies, early = halo(p)
        borders = [jnp.zeros((8, 128), F32)] * 4
        for x in (0, BX - 1):
            plane(x, borders)
        for s in range(2):
            for h in range(2):
                ze[p, s, 8 * h : 8 * h + 8, :] = borders[2 * s + h]
            for k, i in enumerate(XSET[s]):
                start = row_of(i, BX - 1 if s == 0 else 0, 0)
                xs[p, s, k] = field[p][start : start + BY, :]
        for copy in copies[:early]:
            copy.start()
        for x in range(1, BX - 1):
            plane(x, borders)
        for s in range(2):
            for h in range(2):
                zs[p, s, 8 * h : 8 * h + 8, :] = borders[2 * s + h]
            for k, i in enumerate(YSET[s]):
                ys[p, s, k] = field[p][pl.ds(row_of(i, 0, BY - 1 if s == 0 else 0), BX, stride=YPAD), :]
        for copy in copies[early:]:
            copy.start()
        earlier()
        for copy in copies:
            copy.wait_recv()
        lane16 = lax.broadcasted_iota(I32, (BY, 128), 1)
        for s, sign in enumerate((1, -1)):
            for k, i in enumerate(XSET[s]):
                start = row_of(i, -1 if s == 0 else BX, 0)
                field[p][start : start + BY, :] = xr[p, s, k]
            for k, i in enumerate(YSET[s]):
                field[p][pl.ds(row_of(i, 0, -1 if s == 0 else BY), BX, stride=YPAD), :] = yr[p, s, k]
            plane = zr[p, s]
            for t, other in enumerate((1, -1)):
                to, row = (-1, 7) if other > 0 else (BY, 0)
                start = row_of(dist_of(sign, other, 0), -1 if s == 0 else BX, to)
                field[p][start : start + 1, :] = xyr[p, s, t, row : row + 1, :]
                zp[p, s, 8 + to : 9 + to, :] = yzr[p, s, t, row : row + 1, :]
                i = dist_of(other, 0, sign)
                lane = z_lane(s, i, -1 if other > 0 else BX)
                shift = 128 - BX if other > 0 else BX
                plane = jnp.where(lane16 == lane, pltpu.roll(xzr[p, s, t], shift, axis=1), plane)
            zp[p, s, 8:24, :] = plane
        return copies

    def first(x, h):
        return [pops[i, x, 8 * h : 8 * h + 8, :] for i in range(19)]

    def forward_sent():
        @pl.loop(1, groups)
        def _(k):
            forward(k).wait_send()

    def halo_sent(copies):
        for copy in copies:
            copy.wait_send()

    sent = sweep(0, first, forward_sent)
    sent = sweep(1, functools.partial(streamed, 0), functools.partial(halo_sent, sent))

    for x in range(BX):
        incoming = [streamed(1, x, h) for h in range(2)]
        for h in range(2):
            for i in range(19):
                newp[i, x, 8 * h : 8 * h + 8, :] = incoming[h][i]
            density, flow = moments(incoming[h], forces(x, h))
            for c in range(3):
                start = c * SITES + x * BY + 8 * h
                ubuf[start : start + 8, :] = flow[c]

    store = pltpu.make_async_copy(newp, out_hbm, out_sem.at[0])
    store.start()

    turned = [[], []]
    for c in range(3):
        for part, value in enumerate(split(ubuf[c * SITES : (c + 1) * SITES, :].T)):
            turned[part].append(value)
    flow_hi, flow_lo = (jnp.concatenate(part, axis=0) for part in turned)
    flow_all = jnp.concatenate([flow_hi, flow_hi, flow_lo, flow_lo], axis=1)

    def backward(k, dy=0, dz=1):
        return pltpu.make_async_remote_copy(
            src_ref=vbuf.at[k],
            dst_ref=ret_hbm.at[dy * n_gz + dz],
            send_sem=back_send.at[k],
            recv_sem=back_recv.at[k],
            device_id=device(0, -dy, -dz),
            device_id_type=MESH,
        )

    for pair in range(groups // 2 - 1, -1, -1):
        part, start = 2 * pair // PART, 2 * pair % PART * 128
        lanes = slice(start, start + 256)
        block = wxy[part][:, lanes]
        picked = jnp.dot(
            flow_all, jnp.concatenate([block, block], axis=0), preferred_element_type=F32
        )
        weight = wz[part][:, lanes]
        tile = jnp.concatenate([inbuf[2 * pair + e, 6:7, :] for e in range(2)], axis=1)
        tile_z = jnp.broadcast_to(lax.rem(tile.astype(I32), 4), (TZ, 256))
        for c in range(3):
            speed = picked[c * BZ : c * BZ + TZ]
            for z in range(1, BZ // TZ):
                at = c * BZ + z * TZ
                speed = jnp.where(tile_z == z, picked[at : at + TZ], speed)
            speed = speed_scale * jnp.sum(speed * weight, axis=0, keepdims=True)
            for e in range(2):
                vbuf[2 * pair + e, c : c + 1, :] = speed[:, e * 128 : (e + 1) * 128]
        for k in (2 * pair + 1, 2 * pair):
            if k > 0:
                backward(k, *ring[k]).start()

    halo_sent(sent)
    mine = pltpu.make_async_copy(vbuf.at[0], ret_hbm.at[0], out_sem.at[3])
    mine.start()
    for copy in kept:
        copy.wait()
    store.wait()

    @pl.loop(1, groups)
    def _(k):
        backward(k).wait_recv()

    @pl.loop(1, groups)
    def _(k):
        backward(k).wait_send()

    mine.wait()


def hand_over(
    new_hbm,
    ret_hbm,
    rank_hbm,
    rel_hbm,
    new_out,
    vel_out,
    new_ref,
    ret_ref,
    rank_ref,
    rel_ref,
    vel_ref,
    in_sem,
    out_sem,
):
    groups, verts = ret_ref.shape[0], rank_ref.shape[1]
    answers = [(rank_hbm, rank_ref), (rel_hbm, rel_ref), (ret_hbm, ret_ref)]
    answers = [pltpu.make_async_copy(src, dst, in_sem.at[k]) for k, (src, dst) in enumerate(answers)]
    inward = [
        pltpu.make_async_copy(new_hbm.at[part], new_ref.at[part], in_sem.at[3 + k])
        for k, part in enumerate(PIECES)
    ]
    outward = [
        pltpu.make_async_copy(new_ref.at[part], new_out.at[part], out_sem.at[k])
        for k, part in enumerate(PIECES)
    ]
    for copy in answers + inward:
        copy.start()
    answers[0].wait()
    slot_id = lax.broadcasted_iota(I32, (CAP, verts), 0).astype(F32)
    slots = jnp.where(rank_ref[...] == slot_id, 1.0, 0.0).astype(BF16)
    for copy in answers[1:]:
        copy.wait()
    answer = jnp.concatenate([ret_ref[:, c, :] for c in range(3)], axis=0)
    answer_hi = answer.astype(BF16)
    answer_lo = (answer - answer_hi.astype(F32)).astype(BF16)
    both = jnp.concatenate([answer_hi, answer_lo], axis=1)
    found = jnp.dot(both, jnp.concatenate([slots, slots], axis=0), preferred_element_type=F32)
    for k, copy in enumerate(inward):
        copy.wait()
        outward[k].start()
    member = rel_ref[...] == lax.broadcasted_iota(I32, (groups, verts), 0)
    for c in range(3):
        vel_ref[c : c + 1, :] = jnp.sum(
            jnp.where(member, found[c * groups : (c + 1) * groups], 0.0), axis=0, keepdims=True
        )
    outward.append(pltpu.make_async_copy(vel_ref, vel_out, out_sem.at[len(PIECES)]))
    outward[-1].start()
    for copy in outward:
        copy.wait()


def on_device(
    sizes,
    offsets,
    anchor,
    stiffness,
    lattice_block,
    tile_ids,
    populations,
    visc_class,
    fluid_mask,
    tau_table,
):
    groups = sizes[1] * sizes[2]
    verts = offsets.shape[1]
    hbm = pl.BlockSpec(memory_space=pltpu.HBM)
    results = pl.pallas_call(
        functools.partial(kernel, sizes),
        out_shape=(
            jax.ShapeDtypeStruct(populations.shape, F32),
            jax.ShapeDtypeStruct((groups, 4, CAP), F32),
            jax.ShapeDtypeStruct((1, verts), F32),
            jax.ShapeDtypeStruct((1, verts), I32),
        ),
        in_specs=[hbm] * 9,
        out_specs=[hbm] * 4,
        scratch_shapes=[
            pltpu.VMEM((3, verts), F32),
            pltpu.VMEM((3, verts), F32),
            pltpu.VMEM((1, verts), F32),
            pltpu.VMEM((1, verts), I32),
            pltpu.VMEM((1, verts), I32),
            pltpu.SMEM((4,), F32),
            pltpu.VMEM((19, BX, BY, BZ), F32),
            pltpu.VMEM((BX, BY, BZ), I32),
            pltpu.VMEM((BX, BY, BZ), I32),
            pltpu.VMEM((1, verts), F32),
            pltpu.VMEM((1, verts), I32),
            pltpu.VMEM((16, verts), F32),
            pltpu.VMEM((CAP, verts), BF16),
            pltpu.VMEM((groups * 16, verts), BF16),
            pltpu.VMEM((groups, 8, CAP), F32),
            pltpu.VMEM((groups, 8, CAP), F32),
            [pltpu.VMEM((TZ, PART * CAP), F32)] * (groups // PART),
            [pltpu.VMEM((2 * SITES, PART * CAP), BF16)] * (groups // PART),
            [pltpu.VMEM((6 * BZ, PART * CAP), BF16)] * (groups // PART),
            pltpu.VMEM((2 * SITES, 6 * BZ), F32),
            pltpu.VMEM((3 * SITES, BZ), F32),
            pltpu.VMEM((19 * XPAD * YPAD, BZ), F32),
            pltpu.VMEM((19 * XPAD * YPAD, BZ), F32),
            pltpu.VMEM((2, 2, 5, BY, BZ), F32),
            pltpu.VMEM((2, 2, 5, BY, BZ), F32),
            pltpu.VMEM((2, 2, 5, BX, BZ), F32),
            pltpu.VMEM((2, 2, 5, BX, BZ), F32),
            pltpu.VMEM((2, 2, 2, BX, BZ), F32),
            pltpu.VMEM((2, 2, BY, 128), F32),
            pltpu.VMEM((2, 2, BY, 128), F32),
            pltpu.VMEM((2, 2, BY, 128), F32),
            pltpu.VMEM((2, 2, 2, BY, 128), F32),
            pltpu.VMEM((2, 2, 2, 8, 128), F32),
            pltpu.VMEM((2, 2, YPAD, 128), F32),
            pltpu.VMEM((3 * SITES, BZ), F32),
            pltpu.VMEM((19, BX, BY, BZ), F32),
            pltpu.VMEM((groups, 4, CAP), F32),
            pltpu.SemaphoreType.DMA((9,)),
            pltpu.SemaphoreType.DMA((4,)),
            pltpu.SemaphoreType.DMA((groups,)),
            pltpu.SemaphoreType.DMA((groups,)),
            pltpu.SemaphoreType.DMA((2, 18)),
            pltpu.SemaphoreType.DMA((2, 18)),
            pltpu.SemaphoreType.DMA((groups,)),
            pltpu.SemaphoreType.DMA((groups,)),
        ],
        compiler_params=pltpu.CompilerParams(
            collective_id=0, has_side_effects=True, vmem_limit_bytes=60 * 1024 * 1024
        ),
    )(
        offsets,
        anchor,
        stiffness.reshape(1, verts),
        lattice_block.reshape(1, verts),
        tile_ids.reshape(1, verts),
        tau_table,
        populations,
        visc_class,
        fluid_mask,
    )
    return pl.pallas_call(
        hand_over,
        out_shape=[
            jax.ShapeDtypeStruct(populations.shape, F32),
            jax.ShapeDtypeStruct((3, verts), F32),
        ],
        in_specs=[hbm] * 4,
        out_specs=[hbm] * 2,
        scratch_shapes=[
            pltpu.VMEM(populations.shape, F32),
            pltpu.VMEM((groups, 4, CAP), F32),
            pltpu.VMEM((1, verts), F32),
            pltpu.VMEM((1, verts), I32),
            pltpu.VMEM((3, verts), F32),
            pltpu.SemaphoreType.DMA((3 + len(PIECES),)),
            pltpu.SemaphoreType.DMA((len(PIECES) + 1,)),
        ],
        compiler_params=pltpu.CompilerParams(vmem_limit_bytes=60 * 1024 * 1024),
    )(*results)


def solution(mesh):
    placed = (
        P(None, ("gx", "gy", "gz")),
        P(None, ("gx", "gy", "gz")),
        P(("gx", "gy", "gz")),
        P(("gx", "gy", "gz"), None),
        P(("gx", "gy", "gz")),
        P(None, "gx", "gy", "gz"),
        P("gx", "gy", "gz"),
        P("gx", "gy", "gz"),
        P(),
    )
    sizes = tuple(mesh.shape[axis] for axis in ("gx", "gy", "gz"))
    return jax.shard_map(
        functools.partial(on_device, sizes),
        mesh=mesh,
        in_specs=placed,
        out_specs=(P(None, "gx", "gy", "gz"), P(None, ("gx", "gy", "gz"))),
        check_vma=False,
    )
```

```python
import functools

import jax
import jax.numpy as jnp
from jax import lax
from jax.experimental import pallas as pl
from jax.experimental.pallas import tpu as pltpu
from jax.sharding import PartitionSpec as P

MESH = pl.DeviceIdType.MESH
CAP = 128
BX, BY, BZ = 8, 16, 128
SITES = BX * BY
TZ = 32
WIDE = 4
PIECES = [pl.ds(start, min(5, 19 - start)) for start in range(0, 19, 5)]
PARTS = (8, 8, 8, 4, 4)
XPAD, YPAD = BX + 2, 32
F32, BF16, I32 = jnp.float32, jnp.bfloat16, jnp.int32

lattice_velocity = [
    (0, 0, 0),
    (1, 0, 0),
    (-1, 0, 0),
    (0, 1, 0),
    (0, -1, 0),
    (0, 0, 1),
    (0, 0, -1),
    (1, 1, 0),
    (-1, -1, 0),
    (1, -1, 0),
    (-1, 1, 0),
    (1, 0, 1),
    (-1, 0, -1),
    (1, 0, -1),
    (-1, 0, 1),
    (0, 1, 1),
    (0, -1, -1),
    (0, 1, -1),
    (0, -1, 1),
]
lattice_weight = [1.0 / 3.0] + [1.0 / 18.0] * 6 + [1.0 / 36.0] * 12
speed_scale = 20.0
pairs = [(i, i + 1) for i in range(1, 19, 2)]


def crossing(axis, sign):
    return [i for i in range(19) if lattice_velocity[i][axis] == sign]


XSET = [crossing(0, 1), crossing(0, -1)]
YSET = [crossing(1, 1), crossing(1, -1)]


def dist_of(*velocity):
    return lattice_velocity.index(tuple(velocity))


ZPAIRS = [
    (dist_of(cx, cy, 1), dist_of(cx, cy, -1))
    for cx, cy in ((0, 0), (1, 0), (-1, 0), (0, 1), (0, -1))
]


def z_lane(q, x):
    return 2 * (q * XPAD + x + 1)


def row_of(index, x, y):
    return (index * XPAD + x + 1) * YPAD + 8 + y


def moments(f, force):
    density = functools.reduce(lambda a, b: a + b, f)
    inverse = 1.0 / density
    flow = []
    for axis in range(3):
        plus = [f[i] for i in crossing(axis, 1)]
        minus = [f[i] for i in crossing(axis, -1)]
        total = functools.reduce(lambda a, b: a + b, plus) - functools.reduce(lambda a, b: a + b, minus)
        flow.append((total + 0.5 * force[axis]) * inverse)
    return density, flow


def prepare(f, omega, fluid):
    density = functools.reduce(lambda a, b: a + b, f)
    keep = 1.0 - omega
    kept = [None] * 19
    kept[0] = jnp.where(fluid, keep * f[0], f[0])
    for i, j in pairs:
        kept[i] = jnp.where(fluid, keep * f[i], f[j])
        kept[j] = jnp.where(fluid, keep * f[j], f[i])
    momentum = []
    for axis in range(3):
        plus = [f[i] for i in crossing(axis, 1)]
        minus = [f[i] for i in crossing(axis, -1)]
        momentum.append(functools.reduce(lambda a, b: a + b, plus) - functools.reduce(lambda a, b: a + b, minus))
    amount = jnp.where(fluid, omega * density, 0.0)
    gain = jnp.where(fluid, 1.0 - 0.5 * omega, 0.0)
    return kept, [1.0 / density, *momentum, amount, gain]


def complete(kept, values, force):
    inverse, amount, gain = values[0], values[4], values[5]
    flow = [(values[1 + a] + 0.5 * force[a]) * inverse for a in range(3)]
    speed_sq = flow[0] * flow[0] + flow[1] * flow[1] + flow[2] * flow[2]
    work = flow[0] * force[0] + flow[1] * force[1] + flow[2] * force[2]
    base = amount * (1.0 - 1.5 * speed_sq) - (3.0 * gain) * work
    added = added_terms(base, flow, [amount * flow[a] for a in range(3)], [gain * force[a] for a in range(3)])
    return [kept[i] + added[i] for i in range(19)]


def added_terms(base, flow, momentum, push):
    steep = [4.5 * momentum[a] + 9.0 * push[a] for a in range(3)]
    slope = [3.0 * (momentum[a] + push[a]) for a in range(3)]
    added = [lattice_weight[0] * base] + [None] * 18

    def along(values, velocity):
        total = None
        for axis in range(3):
            if velocity[axis]:
                if total is None:
                    total = values[axis] if velocity[axis] > 0 else -values[axis]
                else:
                    total = total + values[axis] if velocity[axis] > 0 else total - values[axis]
        return total

    for i, j in pairs:
        velocity = lattice_velocity[i]
        even = base + along(flow, velocity) * along(steep, velocity)
        odd = along(slope, velocity)
        added[i] = lattice_weight[i] * (even + odd)
        added[j] = lattice_weight[i] * (even - odd)
    return added


def collide(f, force, omega, fluid):
    density, flow = moments(f, force)
    speed_sq = flow[0] * flow[0] + flow[1] * flow[1] + flow[2] * flow[2]
    work = flow[0] * force[0] + flow[1] * force[1] + flow[2] * force[2]
    gain = 1.0 - 0.5 * omega
    keep = 1.0 - omega
    amount = omega * density
    base = amount * (1.0 - 1.5 * speed_sq) - (3.0 * gain) * work
    momentum = [amount * flow[a] for a in range(3)]
    push = [gain * force[a] for a in range(3)]
    added = added_terms(base, flow, momentum, push)
    result = [jnp.where(fluid, keep * f[0] + added[0], f[0])] + [None] * 18
    for i, j in pairs:
        result[i] = jnp.where(fluid, keep * f[i] + added[i], f[j])
        result[j] = jnp.where(fluid, keep * f[j] + added[j], f[i])
    return result


def kernel(
    sizes,
    off_hbm,
    anc_hbm,
    stf_hbm,
    tgt_hbm,
    tid_hbm,
    tau_hbm,
    pop_hbm,
    cls_hbm,
    flu_hbm,
    out_hbm,
    ret_hbm,
    rank_hbm,
    rel_hbm,
    off_ref,
    anc_ref,
    stf_ref,
    tgt_ref,
    tid_ref,
    tau_ref,
    pops,
    cls,
    flu,
    rank_ref,
    rel_ref,
    rows,
    rt,
    lhs,
    outbuf,
    inbuf,
    wz,
    wxy,
    load,
    acc,
    force,
    field0,
    field1,
    xs,
    xr,
    ys,
    yr,
    xyr,
    zs,
    ze,
    zr,
    xzr,
    yzr,
    zp,
    ubuf,
    newp,
    calm,
    vbuf,
    in_sem,
    out_sem,
    fwd_send,
    fwd_recv,
    halo_send,
    halo_recv,
    back_send,
    back_recv,
):
    n_gx, n_gy, n_gz = sizes
    field = (field0, field1)
    groups = n_gy * n_gz
    verts = off_ref.shape[1]
    chunks = verts // 128
    gx, gy, gz = lax.axis_index("gx"), lax.axis_index("gy"), lax.axis_index("gz")

    def device(dx, dy, dz):
        return (
            lax.rem(gx + dx + n_gx, n_gx),
            lax.rem(gy + dy + n_gy, n_gy),
            lax.rem(gz + dz + n_gz, n_gz),
        )

    arguments = [
        (tgt_hbm, tgt_ref),
        (off_hbm, off_ref),
        (anc_hbm, anc_ref),
        (stf_hbm, stf_ref),
        (tid_hbm, tid_ref),
        (tau_hbm, tau_ref),
        (cls_hbm, cls),
        (flu_hbm, flu),
        (pop_hbm, pops),
    ]
    ring = sorted(
        ((dy, dz) for dy in range(n_gy) for dz in range(n_gz)),
        key=lambda at: (min(at[0], n_gy - at[0]) + min(at[1], n_gz - at[1]), at),
    )
    loads = [pltpu.make_async_copy(src, dst, in_sem.at[k]) for k, (src, dst) in enumerate(arguments)]
    barrier = pltpu.get_barrier_semaphore()

    for offset in ring[:0:-1]:
        pl.semaphore_signal(barrier, inc=1, device_id=device(0, *offset), device_id_type=MESH)
    others = [(sx, 0, 0) for sx in (1, -1)]
    others += [(sx, sy, 0) for sx in (1, -1) for sy in (1, -1)]
    others += [(sx, 0, sz) for sx in (1, -1) for sz in (1, -1)]
    for offset in others:
        pl.semaphore_signal(barrier, inc=1, device_id=device(*offset), device_id_type=MESH)

    for copy in loads:
        copy.start()

    loads[0].wait()
    target = tgt_ref[...]
    rel_y = lax.rem(target // n_gz - gy + n_gy, n_gy)
    rel_z = lax.rem(lax.rem(target, n_gz) - gz + n_gz, n_gz)
    rel = rel_y * n_gz + rel_z
    member = rel == lax.broadcasted_iota(I32, (groups, verts), 0)
    member_f = jnp.where(member, 1.0, 0.0).astype(F32)
    stacked = jnp.concatenate([member_f[:, c * 128 : (c + 1) * 128] for c in range(chunks)], axis=0)
    row_id = lax.broadcasted_iota(I32, (128, 256), 0)
    col_id = lax.broadcasted_iota(I32, (128, 256), 1)
    prefix = jnp.where((row_id < col_id) | (col_id >= 128), 1.0, 0.0).astype(BF16)
    counts = jnp.dot(stacked.astype(BF16), prefix, preferred_element_type=F32)
    base = jnp.zeros((groups, 128), F32)
    slot_id = lax.broadcasted_iota(I32, (128, 128), 0).astype(F32)
    for c in range(chunks):
        part = counts[c * groups : (c + 1) * groups]
        rank = jnp.sum(
            member_f[:, c * 128 : (c + 1) * 128] * (part[:, :128] + base), axis=0, keepdims=True
        )
        base = base + part[:, 128:]
        rt[:, c * 128 : (c + 1) * 128] = jnp.where(rank == slot_id, 1.0, 0.0).astype(BF16)
        rank_ref[:, c * 128 : (c + 1) * 128] = rank
    rel_ref[...] = rel
    kept = [
        pltpu.make_async_copy(rank_ref, rank_hbm, out_sem.at[1]),
        pltpu.make_async_copy(rel_ref, rel_hbm, out_sem.at[2]),
    ]
    for copy in kept:
        copy.start()

    def high(value):
        return value.astype(BF16).astype(F32)

    for copy in loads[1:5]:
        copy.wait()
    offs = off_ref[...]
    push = stf_ref[...] * (anc_ref[...] - offs)
    offs_hi = high(offs)
    offs_mid = high(offs - offs_hi)
    push_hi = high(push)
    rows[...] = jnp.zeros((16, verts), F32)
    rows[0:3, :] = offs_hi
    rows[3:6, :] = push_hi
    rows[6:7, :] = tid_ref[...].astype(F32)
    rows[7:8, :] = (offs - offs_hi - offs_mid)[2:3]
    rows[8:11, :] = offs_mid
    rows[11:14, :] = push - push_hi
    for d in range(groups):
        lhs[d * 16 : (d + 1) * 16, :] = jnp.where(rel == d, rows[...], 0.0).astype(BF16)
    packed = lax.dot_general(
        lhs[...], rt[...], (((1,), (1,)), ((), ())), preferred_element_type=F32
    )
    sub8 = lax.broadcasted_iota(I32, (8, 128), 0)
    lane8 = lax.broadcasted_iota(I32, (8, 128), 1)
    for d in range(groups):
        both = packed[d * 16 : d * 16 + 8] + packed[d * 16 + 8 : d * 16 + 16]
        fine = pltpu.roll(both, 3, axis=0)
        outbuf[d] = both + jnp.where(sub8 == 2, fine, 0.0)
    inbuf[0] = outbuf[0]

    pl.semaphore_wait(barrier, groups - 1 + len(others))

    def forward(k, dy=0, dz=1):
        return pltpu.make_async_remote_copy(
            src_ref=outbuf.at[dy * n_gz + dz],
            dst_ref=inbuf.at[k],
            send_sem=fwd_send.at[k],
            recv_sem=fwd_recv.at[k],
            device_id=device(0, dy, dz),
            device_id_type=MESH,
        )

    for k in range(1, groups):
        forward(k, *ring[k]).start()

    for copy in loads[5:]:
        copy.wait()

    taus = [1.0 / jnp.full((8, 128), tau_ref[k], F32) for k in range(4)]

    def site_values(x, h):
        rows_at = slice(8 * h, 8 * h + 8)
        klass = cls[x, rows_at, :]
        omega = jnp.where(
            klass < 2, jnp.where(klass == 0, taus[0], taus[1]), jnp.where(klass == 2, taus[2], taus[3])
        )
        return omega, flu[x, rows_at, :] > 0

    for x in range(BX):
        for h in range(2):
            rows_here = slice(8 * h, 8 * h + 8)
            omega, fluid = site_values(x, h)
            still, values = prepare([pops[i, x, rows_here, :] for i in range(19)], omega, fluid)
            for i in range(19):
                calm[i, x, rows_here, :] = still[i]
            for k in range(6):
                calm[19 + k, x, rows_here, :] = values[k]

    wide = 128 * WIDE
    x_id = lax.broadcasted_iota(I32, (BX, wide), 0)
    y_id = lax.broadcasted_iota(I32, (BY, wide), 0)
    z_half = 0.5 * lax.broadcasted_iota(I32, (TZ, wide), 0).astype(F32)
    third = 1.0 / 1.5

    def split(value):
        top = value.astype(BF16)
        return top, (value - top.astype(F32)).astype(BF16)

    def spread(part, at):
        first = sum(PARTS[:part]) + at * WIDE
        blk = jnp.concatenate([inbuf[first + e] for e in range(WIDE)], axis=1)
        tile = blk[6:7].astype(I32)
        tile_x, tile_y, tile_z = tile // 32, lax.rem(tile // 4, 8), lax.rem(tile, 4)
        dist_x = 2.0 * blk[0:1] - lax.rem(x_id, 2).astype(F32)
        wx = jnp.where(x_id // 2 == tile_x, jnp.maximum(0.0, 1.0 - jnp.abs(dist_x) * third), 0.0)
        dist_y = 2.0 * blk[1:2] - lax.rem(y_id, 2).astype(F32)
        wy = jnp.where(y_id // 2 == tile_y, jnp.maximum(0.0, 1.0 - jnp.abs(dist_y) * third), 0.0)
        weight = jnp.maximum(0.0, 1.0 - jnp.abs(16.0 * blk[2:3] - z_half))
        lanes = slice(at * wide, (at + 1) * wide)
        wz[part][:, lanes] = weight
        for x in range(BX):
            for piece, value in enumerate(split(wx[x : x + 1] * wy)):
                row = piece * SITES + x * BY
                wxy[part][row : row + BY, lanes] = value
        for c in range(3):
            for piece, value in enumerate(split(weight * blk[3 + c : 4 + c])):
                for z in range(BZ // TZ):
                    row = (piece * 3 + c) * BZ + z * TZ
                    load[part][row : row + TZ, lanes] = jnp.where(
                        jnp.broadcast_to(tile_z == z, (TZ, wide)), value, jnp.zeros_like(value)
                    )

    for part, count in enumerate(PARTS):
        start = sum(PARTS[:part])
        for k in range(max(start, 1), start + count):
            forward(k).wait_recv()
        for at in range(count // WIDE):
            spread(part, at)
        product = lax.dot_general(
            wxy[part][...], load[part][...], (((1,), (1,)), ((), ())), preferred_element_type=F32
        )
        if part == 0:
            acc[...] = product
        else:
            acc[...] += product
    for c in range(3):
        here, there = slice(c * BZ, (c + 1) * BZ), slice((3 + c) * BZ, (4 + c) * BZ)
        force[c * SITES : (c + 1) * SITES, :] = (acc[0:SITES, here] + acc[0:SITES, there]) + (
            acc[SITES:, here] + acc[SITES:, there]
        )

    def forces(x, h):
        starts = [c * SITES + x * BY + 8 * h for c in range(3)]
        return [force[start : start + 8, :] for start in starts]

    def messages(p):
        early, late = [], []
        for s, sign in enumerate((1, -1)):
            early.append(((sign, 0, 0), xs.at[p, s], xr.at[p, s]))
            late.append(((0, sign, 0), ys.at[p, s], yr.at[p, s]))
            late.append(((0, 0, sign), zs.at[p], zr.at[p, s]))
            for t, other in enumerate((1, -1)):
                edge = pl.ds(8 if other > 0 else 0, 8)
                spot = XSET[s].index(dist_of(sign, other, 0))
                early.append(((sign, other, 0), xs.at[p, s, spot, edge], xyr.at[p, s, t]))
                early.append(((other, 0, sign), ze.at[p], xzr.at[p, s, t]))
                late.append(((0, other, sign), zs.at[p, edge], yzr.at[p, s, t]))
        hops = lambda message: -sum(abs(v) for v in message[0])
        return sorted(early, key=hops), sorted(late, key=hops)

    def halo(p):
        early, late = messages(p)
        return [
            pltpu.make_async_remote_copy(
                src_ref=src,
                dst_ref=dst,
                send_sem=halo_send.at[p, m],
                recv_sem=halo_recv.at[p, m],
                device_id=device(*offset),
                device_id_type=MESH,
            )
            for m, (offset, src, dst) in enumerate(early + late)
        ], len(early)

    def streamed(p, x, h):
        found = []
        for i in range(19):
            cx, cy, cz = lattice_velocity[i]
            start = row_of(i, x - cx, 8 * h - cy)
            found.append(field[p][start : start + 8, :])
        for q, (up, down) in enumerate(ZPAIRS):
            cx, cy, _ = lattice_velocity[up]
            border = zp[p, 8 + 8 * h - cy : 16 + 8 * h - cy, :]
            border = pltpu.roll(border, 127 - z_lane(q, x - cx), axis=1)
            found[up] = jnp.where(lane8 == 0, border, pltpu.roll(found[up], 1, axis=1))
            found[down] = jnp.where(lane8 == 127, border, pltpu.roll(found[down], 127, axis=1))
        return found

    def sweep(p, source, rule, earlier):
        def plane(x, borders):
            incoming = [source(x, h) for h in range(2)]
            for h in range(2):
                result = rule(incoming[h], x, h)
                for i in range(19):
                    start = row_of(i, x, 8 * h)
                    field[p][start : start + 8, :] = result[i]
                for q, (up, down) in enumerate(ZPAIRS):
                    lane = z_lane(q, x)
                    both = jnp.where(lane8 == 0, result[down], result[up])
                    borders[h] = jnp.where(
                        lane8 // 2 == lane // 2, pltpu.roll(both, lane + 1, axis=1), borders[h]
                    )

        copies, early = halo(p)
        borders = [jnp.zeros((8, 128), F32)] * 2
        for x in (0, BX - 1):
            plane(x, borders)
        for h in range(2):
            ze[p, 8 * h : 8 * h + 8, :] = borders[h]
        for s in range(2):
            for k, i in enumerate(XSET[s]):
                start = row_of(i, BX - 1 if s == 0 else 0, 0)
                xs[p, s, k] = field[p][start : start + BY, :]
        for copy in copies[:early]:
            copy.start()
        for x in range(1, BX - 1):
            plane(x, borders)
        for h in range(2):
            zs[p, 8 * h : 8 * h + 8, :] = borders[h]
        for s in range(2):
            for k, i in enumerate(YSET[s]):
                ys[p, s, k] = field[p][pl.ds(row_of(i, 0, BY - 1 if s == 0 else 0), BX, stride=YPAD), :]
        for copy in copies[early:]:
            copy.start()
        earlier()
        for copy in copies:
            copy.wait_recv()
        lane16 = lax.broadcasted_iota(I32, (BY, 128), 1)
        planes, edges = [], []
        for s, sign in enumerate((1, -1)):
            for k, i in enumerate(XSET[s]):
                start = row_of(i, -1 if s == 0 else BX, 0)
                field[p][start : start + BY, :] = xr[p, s, k]
            for k, i in enumerate(YSET[s]):
                field[p][pl.ds(row_of(i, 0, -1 if s == 0 else BY), BX, stride=YPAD), :] = yr[p, s, k]
            plane_in = pltpu.roll(zr[p, s], sign % 128, axis=1)
            for t, other in enumerate((1, -1)):
                to, row = (-1, 7) if other > 0 else (BY, 0)
                start = row_of(dist_of(sign, other, 0), -1 if s == 0 else BX, to)
                field[p][start : start + 1, :] = xyr[p, s, t, row : row + 1, :]
                edges.append(pltpu.roll(yzr[p, s, t], sign % 128, axis=1)[row : row + 1])
                q = [lattice_velocity[up][0] for up, _ in ZPAIRS].index(other)
                lane = z_lane(q, -1 if other > 0 else BX)
                shift = (sign - 2 * BX * other) % 128
                plane_in = jnp.where(
                    lane16 // 2 == lane // 2, pltpu.roll(xzr[p, s, t], shift, axis=1), plane_in
                )
            planes.append(plane_in)
        zp[p, 8:24, :] = jnp.where(lane16 % 2 == 1, planes[0], planes[1])
        odd = lane16[0:1] % 2 == 1
        zp[p, 7:8, :] = jnp.where(odd, edges[0], edges[2])
        zp[p, 24:25, :] = jnp.where(odd, edges[1], edges[3])
        return copies

    def first(x, h):
        return [calm[i, x, 8 * h : 8 * h + 8, :] for i in range(25)]

    def forward_sent():
        @pl.loop(1, groups)
        def _(k):
            forward(k).wait_send()

    def halo_sent(copies):
        for copy in copies:
            copy.wait_send()

    def second_rule(incoming, x, h):
        omega, fluid = site_values(x, h)
        return collide(incoming, forces(x, h), omega, fluid)

    def first_rule(incoming, x, h):
        return complete(incoming[:19], incoming[19:], forces(x, h))

    sent = sweep(0, first, first_rule, forward_sent)
    sent = sweep(1, functools.partial(streamed, 0), second_rule, functools.partial(halo_sent, sent))

    for x in range(BX):
        incoming = [streamed(1, x, h) for h in range(2)]
        for h in range(2):
            for i in range(19):
                newp[i, x, 8 * h : 8 * h + 8, :] = incoming[h][i]
            density, flow = moments(incoming[h], forces(x, h))
            for c in range(3):
                start = c * SITES + x * BY + 8 * h
                ubuf[start : start + 8, :] = flow[c]

    store = pltpu.make_async_copy(newp, out_hbm, out_sem.at[0])
    store.start()

    turned = [[], []]
    for c in range(3):
        for part, value in enumerate(split(ubuf[c * SITES : (c + 1) * SITES, :].T)):
            turned[part].append(value)
    flow_hi, flow_lo = (jnp.concatenate(part, axis=0) for part in turned)
    flow_all = jnp.concatenate([flow_hi, flow_hi, flow_lo, flow_lo], axis=1)

    def backward(k, dy=0, dz=1):
        return pltpu.make_async_remote_copy(
            src_ref=vbuf.at[k],
            dst_ref=ret_hbm.at[dy * n_gz + dz],
            send_sem=back_send.at[k],
            recv_sem=back_recv.at[k],
            device_id=device(0, -dy, -dz),
            device_id_type=MESH,
        )

    for pair in range(groups // 2 - 1, -1, -1):
        part = max(p for p in range(len(PARTS)) if sum(PARTS[:p]) <= 2 * pair)
        start = (2 * pair - sum(PARTS[:part])) * 128
        lanes = slice(start, start + 256)
        block = wxy[part][:, lanes]
        picked = jnp.dot(
            flow_all, jnp.concatenate([block, block], axis=0), preferred_element_type=F32
        )
        weight = wz[part][:, lanes]
        tile = jnp.concatenate([inbuf[2 * pair + e, 6:7, :] for e in range(2)], axis=1)
        tile_z = jnp.broadcast_to(lax.rem(tile.astype(I32), 4), (TZ, 256))
        for c in range(3):
            speed = picked[c * BZ : c * BZ + TZ]
            for z in range(1, BZ // TZ):
                at = c * BZ + z * TZ
                speed = jnp.where(tile_z == z, picked[at : at + TZ], speed)
            speed = speed_scale * jnp.sum(speed * weight, axis=0, keepdims=True)
            for e in range(2):
                vbuf[2 * pair + e, c : c + 1, :] = speed[:, e * 128 : (e + 1) * 128]
        for k in (2 * pair + 1, 2 * pair):
            if k > 0:
                backward(k, *ring[k]).start()

    halo_sent(sent)
    mine = pltpu.make_async_copy(vbuf.at[0], ret_hbm.at[0], out_sem.at[3])
    mine.start()
    for copy in kept:
        copy.wait()
    store.wait()

    @pl.loop(1, groups)
    def _(k):
        backward(k).wait_recv()

    @pl.loop(1, groups)
    def _(k):
        backward(k).wait_send()

    mine.wait()


def hand_over(
    new_hbm,
    ret_hbm,
    rank_hbm,
    rel_hbm,
    new_out,
    vel_out,
    new_ref,
    ret_ref,
    rank_ref,
    rel_ref,
    vel_ref,
    in_sem,
    out_sem,
):
    groups, verts = ret_ref.shape[0], rank_ref.shape[1]
    answers = [(rank_hbm, rank_ref), (rel_hbm, rel_ref), (ret_hbm, ret_ref)]
    answers = [pltpu.make_async_copy(src, dst, in_sem.at[k]) for k, (src, dst) in enumerate(answers)]
    inward = [
        pltpu.make_async_copy(new_hbm.at[part], new_ref.at[part], in_sem.at[3 + k])
        for k, part in enumerate(PIECES)
    ]
    outward = [
        pltpu.make_async_copy(new_ref.at[part], new_out.at[part], out_sem.at[k])
        for k, part in enumerate(PIECES)
    ]
    for copy in answers + inward:
        copy.start()
    answers[0].wait()
    slot_id = lax.broadcasted_iota(I32, (CAP, verts), 0).astype(F32)
    slots = jnp.where(rank_ref[...] == slot_id, 1.0, 0.0).astype(BF16)
    for copy in answers[1:]:
        copy.wait()
    answer = jnp.concatenate([ret_ref[:, c, :] for c in range(3)], axis=0)
    answer_hi = answer.astype(BF16)
    answer_lo = (answer - answer_hi.astype(F32)).astype(BF16)
    both = jnp.concatenate([answer_hi, answer_lo], axis=1)
    found = jnp.dot(both, jnp.concatenate([slots, slots], axis=0), preferred_element_type=F32)
    for k, copy in enumerate(inward):
        copy.wait()
        outward[k].start()
    member = rel_ref[...] == lax.broadcasted_iota(I32, (groups, verts), 0)
    for c in range(3):
        vel_ref[c : c + 1, :] = jnp.sum(
            jnp.where(member, found[c * groups : (c + 1) * groups], 0.0), axis=0, keepdims=True
        )
    outward.append(pltpu.make_async_copy(vel_ref, vel_out, out_sem.at[len(PIECES)]))
    outward[-1].start()
    for copy in outward:
        copy.wait()


def on_device(
    sizes,
    offsets,
    anchor,
    stiffness,
    lattice_block,
    tile_ids,
    populations,
    visc_class,
    fluid_mask,
    tau_table,
):
    groups = sizes[1] * sizes[2]
    verts = offsets.shape[1]
    hbm = pl.BlockSpec(memory_space=pltpu.HBM)
    results = pl.pallas_call(
        functools.partial(kernel, sizes),
        out_shape=(
            jax.ShapeDtypeStruct(populations.shape, F32),
            jax.ShapeDtypeStruct((groups, 4, CAP), F32),
            jax.ShapeDtypeStruct((1, verts), F32),
            jax.ShapeDtypeStruct((1, verts), I32),
        ),
        in_specs=[hbm] * 9,
        out_specs=[hbm] * 4,
        scratch_shapes=[
            pltpu.VMEM((3, verts), F32),
            pltpu.VMEM((3, verts), F32),
            pltpu.VMEM((1, verts), F32),
            pltpu.VMEM((1, verts), I32),
            pltpu.VMEM((1, verts), I32),
            pltpu.SMEM((4,), F32),
            pltpu.VMEM((19, BX, BY, BZ), F32),
            pltpu.VMEM((BX, BY, BZ), I32),
            pltpu.VMEM((BX, BY, BZ), I32),
            pltpu.VMEM((1, verts), F32),
            pltpu.VMEM((1, verts), I32),
            pltpu.VMEM((16, verts), F32),
            pltpu.VMEM((CAP, verts), BF16),
            pltpu.VMEM((groups * 16, verts), BF16),
            pltpu.VMEM((groups, 8, CAP), F32),
            pltpu.VMEM((groups, 8, CAP), F32),
            [pltpu.VMEM((TZ, count * CAP), F32) for count in PARTS],
            [pltpu.VMEM((2 * SITES, count * CAP), BF16) for count in PARTS],
            [pltpu.VMEM((6 * BZ, count * CAP), BF16) for count in PARTS],
            pltpu.VMEM((2 * SITES, 6 * BZ), F32),
            pltpu.VMEM((3 * SITES, BZ), F32),
            pltpu.VMEM((19 * XPAD * YPAD, BZ), F32),
            pltpu.VMEM((19 * XPAD * YPAD, BZ), F32),
            pltpu.VMEM((2, 2, 5, BY, BZ), F32),
            pltpu.VMEM((2, 2, 5, BY, BZ), F32),
            pltpu.VMEM((2, 2, 5, BX, BZ), F32),
            pltpu.VMEM((2, 2, 5, BX, BZ), F32),
            pltpu.VMEM((2, 2, 2, BX, BZ), F32),
            pltpu.VMEM((2, BY, 128), F32),
            pltpu.VMEM((2, BY, 128), F32),
            pltpu.VMEM((2, 2, BY, 128), F32),
            pltpu.VMEM((2, 2, 2, BY, 128), F32),
            pltpu.VMEM((2, 2, 2, 8, 128), F32),
            pltpu.VMEM((2, YPAD, 128), F32),
            pltpu.VMEM((3 * SITES, BZ), F32),
            pltpu.VMEM((19, BX, BY, BZ), F32),
            pltpu.VMEM((25, BX, BY, BZ), F32),
            pltpu.VMEM((groups, 4, CAP), F32),
            pltpu.SemaphoreType.DMA((9,)),
            pltpu.SemaphoreType.DMA((4,)),
            pltpu.SemaphoreType.DMA((groups,)),
            pltpu.SemaphoreType.DMA((groups,)),
            pltpu.SemaphoreType.DMA((2, 18)),
            pltpu.SemaphoreType.DMA((2, 18)),
            pltpu.SemaphoreType.DMA((groups,)),
            pltpu.SemaphoreType.DMA((groups,)),
        ],
        compiler_params=pltpu.CompilerParams(
            collective_id=0, has_side_effects=True, vmem_limit_bytes=60 * 1024 * 1024
        ),
    )(
        offsets,
        anchor,
        stiffness.reshape(1, verts),
        lattice_block.reshape(1, verts),
        tile_ids.reshape(1, verts),
        tau_table,
        populations,
        visc_class,
        fluid_mask,
    )
    return pl.pallas_call(
        hand_over,
        out_shape=[
            jax.ShapeDtypeStruct(populations.shape, F32),
            jax.ShapeDtypeStruct((3, verts), F32),
        ],
        in_specs=[hbm] * 4,
        out_specs=[hbm] * 2,
        scratch_shapes=[
            pltpu.VMEM(populations.shape, F32),
            pltpu.VMEM((groups, 4, CAP), F32),
            pltpu.VMEM((1, verts), F32),
            pltpu.VMEM((1, verts), I32),
            pltpu.VMEM((3, verts), F32),
            pltpu.SemaphoreType.DMA((3 + len(PIECES),)),
            pltpu.SemaphoreType.DMA((len(PIECES) + 1,)),
        ],
        compiler_params=pltpu.CompilerParams(vmem_limit_bytes=60 * 1024 * 1024),
    )(*results)


def solution(mesh):
    placed = (
        P(None, ("gx", "gy", "gz")),
        P(None, ("gx", "gy", "gz")),
        P(("gx", "gy", "gz")),
        P(("gx", "gy", "gz"), None),
        P(("gx", "gy", "gz")),
        P(None, "gx", "gy", "gz"),
        P("gx", "gy", "gz"),
        P("gx", "gy", "gz"),
        P(),
    )
    sizes = tuple(mesh.shape[axis] for axis in ("gx", "gy", "gz"))
    return jax.shard_map(
        functools.partial(on_device, sizes),
        mesh=mesh,
        in_specs=placed,
        out_specs=(P(None, "gx", "gy", "gz"), P(None, ("gx", "gy", "gz"))),
        check_vma=False,
    )
```

```python
import functools

import jax
import jax.numpy as jnp
from jax import lax
from jax.experimental import pallas as pl
from jax.experimental.pallas import tpu as pltpu
from jax.sharding import PartitionSpec as P

MESH = pl.DeviceIdType.MESH
CAP = 128
BX, BY, BZ = 8, 16, 128
SITES = BX * BY
TZ = 32
WIDE = 4
PIECES = [pl.ds(start, min(5, 19 - start)) for start in range(0, 19, 5)]
PARTS = (4, 4, 4, 4, 4, 4, 4, 4)
XPAD, YPAD = BX + 2, 32
F32, BF16, I32 = jnp.float32, jnp.bfloat16, jnp.int32

lattice_velocity = [
    (0, 0, 0),
    (1, 0, 0),
    (-1, 0, 0),
    (0, 1, 0),
    (0, -1, 0),
    (0, 0, 1),
    (0, 0, -1),
    (1, 1, 0),
    (-1, -1, 0),
    (1, -1, 0),
    (-1, 1, 0),
    (1, 0, 1),
    (-1, 0, -1),
    (1, 0, -1),
    (-1, 0, 1),
    (0, 1, 1),
    (0, -1, -1),
    (0, 1, -1),
    (0, -1, 1),
]
lattice_weight = [1.0 / 3.0] + [1.0 / 18.0] * 6 + [1.0 / 36.0] * 12
speed_scale = 20.0
pairs = [(i, i + 1) for i in range(1, 19, 2)]


def crossing(axis, sign):
    return [i for i in range(19) if lattice_velocity[i][axis] == sign]


XSET = [crossing(0, 1), crossing(0, -1)]
YSET = [crossing(1, 1), crossing(1, -1)]


def dist_of(*velocity):
    return lattice_velocity.index(tuple(velocity))


ZPAIRS = [
    (dist_of(cx, cy, 1), dist_of(cx, cy, -1))
    for cx, cy in ((0, 0), (1, 0), (-1, 0), (0, 1), (0, -1))
]


def z_lane(q, x):
    return 2 * (q * XPAD + x + 1)


def row_of(index, x, y):
    return (index * XPAD + x + 1) * YPAD + 8 + y


def moments(f, force):
    density = functools.reduce(lambda a, b: a + b, f)
    inverse = 1.0 / density
    flow = []
    for axis in range(3):
        plus = [f[i] for i in crossing(axis, 1)]
        minus = [f[i] for i in crossing(axis, -1)]
        total = functools.reduce(lambda a, b: a + b, plus) - functools.reduce(lambda a, b: a + b, minus)
        flow.append((total + 0.5 * force[axis]) * inverse)
    return density, flow


def prepare(f, omega, fluid):
    density = functools.reduce(lambda a, b: a + b, f)
    keep = 1.0 - omega
    kept = [None] * 19
    kept[0] = jnp.where(fluid, keep * f[0], f[0])
    for i, j in pairs:
        kept[i] = jnp.where(fluid, keep * f[i], f[j])
        kept[j] = jnp.where(fluid, keep * f[j], f[i])
    momentum = []
    for axis in range(3):
        plus = [f[i] for i in crossing(axis, 1)]
        minus = [f[i] for i in crossing(axis, -1)]
        momentum.append(functools.reduce(lambda a, b: a + b, plus) - functools.reduce(lambda a, b: a + b, minus))
    amount = jnp.where(fluid, omega * density, 0.0)
    gain = jnp.where(fluid, 1.0 - 0.5 * omega, 0.0)
    return kept, [1.0 / density, *momentum, amount, gain]


def complete(kept, values, force):
    inverse, amount, gain = values[0], values[4], values[5]
    flow = [(values[1 + a] + 0.5 * force[a]) * inverse for a in range(3)]
    speed_sq = flow[0] * flow[0] + flow[1] * flow[1] + flow[2] * flow[2]
    work = flow[0] * force[0] + flow[1] * force[1] + flow[2] * force[2]
    base = amount * (1.0 - 1.5 * speed_sq) - (3.0 * gain) * work
    added = added_terms(base, flow, [amount * flow[a] for a in range(3)], [gain * force[a] for a in range(3)])
    return [kept[i] + added[i] for i in range(19)]


def added_terms(base, flow, momentum, push):
    steep = [4.5 * momentum[a] + 9.0 * push[a] for a in range(3)]
    slope = [3.0 * (momentum[a] + push[a]) for a in range(3)]
    added = [lattice_weight[0] * base] + [None] * 18

    def along(values, velocity):
        total = None
        for axis in range(3):
            if velocity[axis]:
                if total is None:
                    total = values[axis] if velocity[axis] > 0 else -values[axis]
                else:
                    total = total + values[axis] if velocity[axis] > 0 else total - values[axis]
        return total

    for i, j in pairs:
        velocity = lattice_velocity[i]
        even = base + along(flow, velocity) * along(steep, velocity)
        odd = along(slope, velocity)
        added[i] = lattice_weight[i] * (even + odd)
        added[j] = lattice_weight[i] * (even - odd)
    return added


def collide(f, force, omega, fluid):
    density, flow = moments(f, force)
    speed_sq = flow[0] * flow[0] + flow[1] * flow[1] + flow[2] * flow[2]
    work = flow[0] * force[0] + flow[1] * force[1] + flow[2] * force[2]
    gain = 1.0 - 0.5 * omega
    keep = 1.0 - omega
    amount = omega * density
    base = amount * (1.0 - 1.5 * speed_sq) - (3.0 * gain) * work
    momentum = [amount * flow[a] for a in range(3)]
    push = [gain * force[a] for a in range(3)]
    added = added_terms(base, flow, momentum, push)
    result = [jnp.where(fluid, keep * f[0] + added[0], f[0])] + [None] * 18
    for i, j in pairs:
        result[i] = jnp.where(fluid, keep * f[i] + added[i], f[j])
        result[j] = jnp.where(fluid, keep * f[j] + added[j], f[i])
    return result


def kernel(
    sizes,
    off_hbm,
    anc_hbm,
    stf_hbm,
    tgt_hbm,
    tid_hbm,
    tau_hbm,
    pop_hbm,
    cls_hbm,
    flu_hbm,
    out_hbm,
    ret_hbm,
    rank_hbm,
    rel_hbm,
    off_ref,
    anc_ref,
    stf_ref,
    tgt_ref,
    tid_ref,
    tau_ref,
    pops,
    cls,
    flu,
    rank_ref,
    rel_ref,
    rows,
    rt,
    lhs,
    outbuf,
    inbuf,
    wz,
    wxy,
    load,
    acc,
    force,
    field0,
    field1,
    xs,
    xr,
    ys,
    yr,
    xyr,
    zs,
    ze,
    zr,
    xzr,
    yzr,
    zp,
    ubuf,
    newp,
    calm,
    vbuf,
    in_sem,
    out_sem,
    fwd_send,
    fwd_recv,
    halo_send,
    halo_recv,
    back_send,
    back_recv,
):
    n_gx, n_gy, n_gz = sizes
    field = (field0, field1)
    groups = n_gy * n_gz
    verts = off_ref.shape[1]
    chunks = verts // 128
    gx, gy, gz = lax.axis_index("gx"), lax.axis_index("gy"), lax.axis_index("gz")

    def device(dx, dy, dz):
        return (
            lax.rem(gx + dx + n_gx, n_gx),
            lax.rem(gy + dy + n_gy, n_gy),
            lax.rem(gz + dz + n_gz, n_gz),
        )

    arguments = [
        (tgt_hbm, tgt_ref),
        (off_hbm, off_ref),
        (anc_hbm, anc_ref),
        (stf_hbm, stf_ref),
        (tid_hbm, tid_ref),
        (tau_hbm, tau_ref),
        (cls_hbm, cls),
        (flu_hbm, flu),
        (pop_hbm, pops),
    ]
    ring = sorted(
        ((dy, dz) for dy in range(n_gy) for dz in range(n_gz)),
        key=lambda at: (min(at[0], n_gy - at[0]) + min(at[1], n_gz - at[1]), at),
    )
    loads = [pltpu.make_async_copy(src, dst, in_sem.at[k]) for k, (src, dst) in enumerate(arguments)]
    barrier = pltpu.get_barrier_semaphore()

    for offset in ring[:0:-1]:
        pl.semaphore_signal(barrier, inc=1, device_id=device(0, *offset), device_id_type=MESH)
    others = [(sx, 0, 0) for sx in (1, -1)]
    others += [(sx, sy, 0) for sx in (1, -1) for sy in (1, -1)]
    others += [(sx, 0, sz) for sx in (1, -1) for sz in (1, -1)]
    for offset in others:
        pl.semaphore_signal(barrier, inc=1, device_id=device(*offset), device_id_type=MESH)

    for copy in loads:
        copy.start()

    loads[0].wait()
    target = tgt_ref[...]
    rel_y = lax.rem(target // n_gz - gy + n_gy, n_gy)
    rel_z = lax.rem(lax.rem(target, n_gz) - gz + n_gz, n_gz)
    rel = rel_y * n_gz + rel_z
    member = rel == lax.broadcasted_iota(I32, (groups, verts), 0)
    member_f = jnp.where(member, 1.0, 0.0).astype(F32)
    stacked = jnp.concatenate([member_f[:, c * 128 : (c + 1) * 128] for c in range(chunks)], axis=0)
    row_id = lax.broadcasted_iota(I32, (128, 256), 0)
    col_id = lax.broadcasted_iota(I32, (128, 256), 1)
    prefix = jnp.where((row_id < col_id) | (col_id >= 128), 1.0, 0.0).astype(BF16)
    counts = jnp.dot(stacked.astype(BF16), prefix, preferred_element_type=F32)
    base = jnp.zeros((groups, 128), F32)
    slot_id = lax.broadcasted_iota(I32, (128, 128), 0).astype(F32)
    for c in range(chunks):
        part = counts[c * groups : (c + 1) * groups]
        rank = jnp.sum(
            member_f[:, c * 128 : (c + 1) * 128] * (part[:, :128] + base), axis=0, keepdims=True
        )
        base = base + part[:, 128:]
        rt[:, c * 128 : (c + 1) * 128] = jnp.where(rank == slot_id, 1.0, 0.0).astype(BF16)
        rank_ref[:, c * 128 : (c + 1) * 128] = rank
    rel_ref[...] = rel
    kept = [
        pltpu.make_async_copy(rank_ref, rank_hbm, out_sem.at[1]),
        pltpu.make_async_copy(rel_ref, rel_hbm, out_sem.at[2]),
    ]
    for copy in kept:
        copy.start()

    def high(value):
        return value.astype(BF16).astype(F32)

    for copy in loads[1:5]:
        copy.wait()
    offs = off_ref[...]
    push = stf_ref[...] * (anc_ref[...] - offs)
    offs_hi = high(offs)
    offs_mid = high(offs - offs_hi)
    push_hi = high(push)
    rows[...] = jnp.zeros((16, verts), F32)
    rows[0:3, :] = offs_hi
    rows[3:6, :] = push_hi
    rows[6:7, :] = tid_ref[...].astype(F32)
    rows[7:8, :] = (offs - offs_hi - offs_mid)[2:3]
    rows[8:11, :] = offs_mid
    rows[11:14, :] = push - push_hi
    for d in range(groups):
        lhs[d * 16 : (d + 1) * 16, :] = jnp.where(rel == d, rows[...], 0.0).astype(BF16)
    packed = lax.dot_general(
        lhs[...], rt[...], (((1,), (1,)), ((), ())), preferred_element_type=F32
    )
    sub8 = lax.broadcasted_iota(I32, (8, 128), 0)
    lane8 = lax.broadcasted_iota(I32, (8, 128), 1)
    for d in range(groups):
        both = packed[d * 16 : d * 16 + 8] + packed[d * 16 + 8 : d * 16 + 16]
        fine = pltpu.roll(both, 3, axis=0)
        outbuf[d] = both + jnp.where(sub8 == 2, fine, 0.0)
    inbuf[0] = outbuf[0]

    pl.semaphore_wait(barrier, groups - 1 + len(others))

    def forward(k, dy=0, dz=1):
        return pltpu.make_async_remote_copy(
            src_ref=outbuf.at[dy * n_gz + dz],
            dst_ref=inbuf.at[k],
            send_sem=fwd_send.at[k],
            recv_sem=fwd_recv.at[k],
            device_id=device(0, dy, dz),
            device_id_type=MESH,
        )

    for k in range(1, groups):
        forward(k, *ring[k]).start()

    for copy in loads[5:]:
        copy.wait()

    taus = [1.0 / jnp.full((8, 128), tau_ref[k], F32) for k in range(4)]

    def site_values(x, h):
        rows_at = slice(8 * h, 8 * h + 8)
        klass = cls[x, rows_at, :]
        omega = jnp.where(
            klass < 2, jnp.where(klass == 0, taus[0], taus[1]), jnp.where(klass == 2, taus[2], taus[3])
        )
        return omega, flu[x, rows_at, :] > 0

    for x in range(BX):
        for h in range(2):
            rows_here = slice(8 * h, 8 * h + 8)
            omega, fluid = site_values(x, h)
            still, values = prepare([pops[i, x, rows_here, :] for i in range(19)], omega, fluid)
            for i in range(19):
                calm[i, x, rows_here, :] = still[i]
            for k in range(6):
                calm[19 + k, x, rows_here, :] = values[k]

    wide = 128 * WIDE
    x_id = lax.broadcasted_iota(I32, (BX, wide), 0)
    y_id = lax.broadcasted_iota(I32, (BY, wide), 0)
    z_half = 0.5 * lax.broadcasted_iota(I32, (TZ, wide), 0).astype(F32)
    third = 1.0 / 1.5

    def split(value):
        top = value.astype(BF16)
        return top, (value - top.astype(F32)).astype(BF16)

    def spread(part, at):
        first = sum(PARTS[:part]) + at * WIDE
        blk = jnp.concatenate([inbuf[first + e] for e in range(WIDE)], axis=1)
        tile = blk[6:7].astype(I32)
        tile_x, tile_y, tile_z = tile // 32, lax.rem(tile // 4, 8), lax.rem(tile, 4)
        dist_x = 2.0 * blk[0:1] - lax.rem(x_id, 2).astype(F32)
        wx = jnp.where(x_id // 2 == tile_x, jnp.maximum(0.0, 1.0 - jnp.abs(dist_x) * third), 0.0)
        dist_y = 2.0 * blk[1:2] - lax.rem(y_id, 2).astype(F32)
        wy = jnp.where(y_id // 2 == tile_y, jnp.maximum(0.0, 1.0 - jnp.abs(dist_y) * third), 0.0)
        weight = jnp.maximum(0.0, 1.0 - jnp.abs(16.0 * blk[2:3] - z_half))
        lanes = slice(at * wide, (at + 1) * wide)
        wz[part][:, lanes] = weight
        for x in range(BX):
            for piece, value in enumerate(split(wx[x : x + 1] * wy)):
                row = piece * SITES + x * BY
                wxy[part][row : row + BY, lanes] = value
        for c in range(3):
            for piece, value in enumerate(split(weight * blk[3 + c : 4 + c])):
                for z in range(BZ // TZ):
                    row = (piece * 3 + c) * BZ + z * TZ
                    load[part][row : row + TZ, lanes] = jnp.where(
                        jnp.broadcast_to(tile_z == z, (TZ, wide)), value, jnp.zeros_like(value)
                    )

    for part, count in enumerate(PARTS):
        start = sum(PARTS[:part])
        for k in range(max(start, 1), start + count):
            forward(k).wait_recv()
        for at in range(count // WIDE):
            spread(part, at)
        product = lax.dot_general(
            wxy[part][...], load[part][...], (((1,), (1,)), ((), ())), preferred_element_type=F32
        )
        if part == 0:
            acc[...] = product
        else:
            acc[...] += product
    for c in range(3):
        here, there = slice(c * BZ, (c + 1) * BZ), slice((3 + c) * BZ, (4 + c) * BZ)
        force[c * SITES : (c + 1) * SITES, :] = (acc[0:SITES, here] + acc[0:SITES, there]) + (
            acc[SITES:, here] + acc[SITES:, there]
        )

    def forces(x, h):
        starts = [c * SITES + x * BY + 8 * h for c in range(3)]
        return [force[start : start + 8, :] for start in starts]

    def messages(p):
        early, late = [], []
        for s, sign in enumerate((1, -1)):
            early.append(((sign, 0, 0), xs.at[p, s], xr.at[p, s]))
            late.append(((0, sign, 0), ys.at[p, s], yr.at[p, s]))
            late.append(((0, 0, sign), zs.at[p], zr.at[p, s]))
            for t, other in enumerate((1, -1)):
                edge = pl.ds(8 if other > 0 else 0, 8)
                spot = XSET[s].index(dist_of(sign, other, 0))
                early.append(((sign, other, 0), xs.at[p, s, spot, edge], xyr.at[p, s, t]))
                early.append(((other, 0, sign), ze.at[p], xzr.at[p, s, t]))
                late.append(((0, other, sign), zs.at[p, edge], yzr.at[p, s, t]))
        hops = lambda message: -sum(abs(v) for v in message[0])
        return sorted(early, key=hops), sorted(late, key=hops)

    def halo(p):
        early, late = messages(p)
        return [
            pltpu.make_async_remote_copy(
                src_ref=src,
                dst_ref=dst,
                send_sem=halo_send.at[p, m],
                recv_sem=halo_recv.at[p, m],
                device_id=device(*offset),
                device_id_type=MESH,
            )
            for m, (offset, src, dst) in enumerate(early + late)
        ], len(early)

    def streamed(p, x, h):
        found = []
        for i in range(19):
            cx, cy, cz = lattice_velocity[i]
            start = row_of(i, x - cx, 8 * h - cy)
            found.append(field[p][start : start + 8, :])
        for q, (up, down) in enumerate(ZPAIRS):
            cx, cy, _ = lattice_velocity[up]
            border = zp[p, 8 + 8 * h - cy : 16 + 8 * h - cy, :]
            border = pltpu.roll(border, 127 - z_lane(q, x - cx), axis=1)
            found[up] = jnp.where(lane8 == 0, border, pltpu.roll(found[up], 1, axis=1))
            found[down] = jnp.where(lane8 == 127, border, pltpu.roll(found[down], 127, axis=1))
        return found

    def sweep(p, source, rule, earlier):
        def plane(x, borders):
            incoming = [source(x, h) for h in range(2)]
            for h in range(2):
                result = rule(incoming[h], x, h)
                for i in range(19):
                    start = row_of(i, x, 8 * h)
                    field[p][start : start + 8, :] = result[i]
                for q, (up, down) in enumerate(ZPAIRS):
                    lane = z_lane(q, x)
                    both = jnp.where(lane8 == 0, result[down], result[up])
                    borders[h] = jnp.where(
                        lane8 // 2 == lane // 2, pltpu.roll(both, lane + 1, axis=1), borders[h]
                    )

        copies, early = halo(p)
        borders = [jnp.zeros((8, 128), F32)] * 2
        for x in (0, BX - 1):
            plane(x, borders)
        for h in range(2):
            ze[p, 8 * h : 8 * h + 8, :] = borders[h]
        for s in range(2):
            for k, i in enumerate(XSET[s]):
                start = row_of(i, BX - 1 if s == 0 else 0, 0)
                xs[p, s, k] = field[p][start : start + BY, :]
        for copy in copies[:early]:
            copy.start()
        for x in range(1, BX - 1):
            plane(x, borders)
        for h in range(2):
            zs[p, 8 * h : 8 * h + 8, :] = borders[h]
        for s in range(2):
            for k, i in enumerate(YSET[s]):
                ys[p, s, k] = field[p][pl.ds(row_of(i, 0, BY - 1 if s == 0 else 0), BX, stride=YPAD), :]
        for copy in copies[early:]:
            copy.start()
        earlier()
        for copy in copies:
            copy.wait_recv()
        lane16 = lax.broadcasted_iota(I32, (BY, 128), 1)
        planes, edges = [], []
        for s, sign in enumerate((1, -1)):
            for k, i in enumerate(XSET[s]):
                start = row_of(i, -1 if s == 0 else BX, 0)
                field[p][start : start + BY, :] = xr[p, s, k]
            for k, i in enumerate(YSET[s]):
                field[p][pl.ds(row_of(i, 0, -1 if s == 0 else BY), BX, stride=YPAD), :] = yr[p, s, k]
            plane_in = pltpu.roll(zr[p, s], sign % 128, axis=1)
            for t, other in enumerate((1, -1)):
                to, row = (-1, 7) if other > 0 else (BY, 0)
                start = row_of(dist_of(sign, other, 0), -1 if s == 0 else BX, to)
                field[p][start : start + 1, :] = xyr[p, s, t, row : row + 1, :]
                edges.append(pltpu.roll(yzr[p, s, t], sign % 128, axis=1)[row : row + 1])
                q = [lattice_velocity[up][0] for up, _ in ZPAIRS].index(other)
                lane = z_lane(q, -1 if other > 0 else BX)
                shift = (sign - 2 * BX * other) % 128
                plane_in = jnp.where(
                    lane16 // 2 == lane // 2, pltpu.roll(xzr[p, s, t], shift, axis=1), plane_in
                )
            planes.append(plane_in)
        zp[p, 8:24, :] = jnp.where(lane16 % 2 == 1, planes[0], planes[1])
        odd = lane16[0:1] % 2 == 1
        zp[p, 7:8, :] = jnp.where(odd, edges[0], edges[2])
        zp[p, 24:25, :] = jnp.where(odd, edges[1], edges[3])
        return copies

    def first(x, h):
        return [calm[i, x, 8 * h : 8 * h + 8, :] for i in range(25)]

    def forward_sent():
        @pl.loop(1, groups)
        def _(k):
            forward(k).wait_send()

    def halo_sent(copies):
        for copy in copies:
            copy.wait_send()

    def second_rule(incoming, x, h):
        omega, fluid = site_values(x, h)
        return collide(incoming, forces(x, h), omega, fluid)

    def first_rule(incoming, x, h):
        return complete(incoming[:19], incoming[19:], forces(x, h))

    sent = sweep(0, first, first_rule, lambda: None)
    earlier_sent = sent
    sent = sweep(1, functools.partial(streamed, 0), second_rule, lambda: (forward_sent(), halo_sent(earlier_sent)))

    for x in range(BX):
        incoming = [streamed(1, x, h) for h in range(2)]
        for h in range(2):
            for i in range(19):
                newp[i, x, 8 * h : 8 * h + 8, :] = incoming[h][i]
            density, flow = moments(incoming[h], forces(x, h))
            for c in range(3):
                start = c * SITES + x * BY + 8 * h
                ubuf[start : start + 8, :] = flow[c]

    store = pltpu.make_async_copy(newp, out_hbm, out_sem.at[0])
    store.start()

    turned = [[], []]
    for c in range(3):
        for part, value in enumerate(split(ubuf[c * SITES : (c + 1) * SITES, :].T)):
            turned[part].append(value)
    flow_hi, flow_lo = (jnp.concatenate(part, axis=0) for part in turned)
    flow_all = jnp.concatenate([flow_hi, flow_hi, flow_lo, flow_lo], axis=1)

    def backward(k, dy=0, dz=1):
        return pltpu.make_async_remote_copy(
            src_ref=vbuf.at[k],
            dst_ref=ret_hbm.at[dy * n_gz + dz],
            send_sem=back_send.at[k],
            recv_sem=back_recv.at[k],
            device_id=device(0, -dy, -dz),
            device_id_type=MESH,
        )

    for pair in range(groups // 2 - 1, -1, -1):
        part = max(p for p in range(len(PARTS)) if sum(PARTS[:p]) <= 2 * pair)
        start = (2 * pair - sum(PARTS[:part])) * 128
        lanes = slice(start, start + 256)
        block = wxy[part][:, lanes]
        picked = jnp.dot(
            flow_all, jnp.concatenate([block, block], axis=0), preferred_element_type=F32
        )
        weight = wz[part][:, lanes]
        tile = jnp.concatenate([inbuf[2 * pair + e, 6:7, :] for e in range(2)], axis=1)
        tile_z = jnp.broadcast_to(lax.rem(tile.astype(I32), 4), (TZ, 256))
        for c in range(3):
            speed = picked[c * BZ : c * BZ + TZ]
            for z in range(1, BZ // TZ):
                at = c * BZ + z * TZ
                speed = jnp.where(tile_z == z, picked[at : at + TZ], speed)
            speed = speed_scale * jnp.sum(speed * weight, axis=0, keepdims=True)
            for e in range(2):
                vbuf[2 * pair + e, c : c + 1, :] = speed[:, e * 128 : (e + 1) * 128]
        for k in (2 * pair + 1, 2 * pair):
            if k > 0:
                backward(k, *ring[k]).start()

    halo_sent(sent)
    mine = pltpu.make_async_copy(vbuf.at[0], ret_hbm.at[0], out_sem.at[3])
    mine.start()
    for copy in kept:
        copy.wait()
    store.wait()

    @pl.loop(1, groups)
    def _(k):
        backward(k).wait_send()

    @pl.loop(1, groups)
    def _(k):
        backward(k).wait_recv()

    mine.wait()


def hand_over(
    new_hbm,
    ret_hbm,
    rank_hbm,
    rel_hbm,
    new_out,
    vel_out,
    new_ref,
    ret_ref,
    rank_ref,
    rel_ref,
    vel_ref,
    in_sem,
    out_sem,
):
    groups, verts = ret_ref.shape[0], rank_ref.shape[1]
    answers = [(rank_hbm, rank_ref), (rel_hbm, rel_ref), (ret_hbm, ret_ref)]
    answers = [pltpu.make_async_copy(src, dst, in_sem.at[k]) for k, (src, dst) in enumerate(answers)]
    inward = [
        pltpu.make_async_copy(new_hbm.at[part], new_ref.at[part], in_sem.at[3 + k])
        for k, part in enumerate(PIECES)
    ]
    outward = [
        pltpu.make_async_copy(new_ref.at[part], new_out.at[part], out_sem.at[k])
        for k, part in enumerate(PIECES)
    ]
    for copy in answers + inward:
        copy.start()
    answers[0].wait()
    slot_id = lax.broadcasted_iota(I32, (CAP, verts), 0).astype(F32)
    slots = jnp.where(rank_ref[...] == slot_id, 1.0, 0.0).astype(BF16)
    for copy in answers[1:]:
        copy.wait()
    answer = jnp.concatenate([ret_ref[:, c, :] for c in range(3)], axis=0)
    answer_hi = answer.astype(BF16)
    answer_lo = (answer - answer_hi.astype(F32)).astype(BF16)
    both = jnp.concatenate([answer_hi, answer_lo], axis=1)
    found = jnp.dot(both, jnp.concatenate([slots, slots], axis=0), preferred_element_type=F32)
    for k, copy in enumerate(inward):
        copy.wait()
        outward[k].start()
    member = rel_ref[...] == lax.broadcasted_iota(I32, (groups, verts), 0)
    for c in range(3):
        vel_ref[c : c + 1, :] = jnp.sum(
            jnp.where(member, found[c * groups : (c + 1) * groups], 0.0), axis=0, keepdims=True
        )
    outward.append(pltpu.make_async_copy(vel_ref, vel_out, out_sem.at[len(PIECES)]))
    outward[-1].start()
    for copy in outward:
        copy.wait()


def on_device(
    sizes,
    offsets,
    anchor,
    stiffness,
    lattice_block,
    tile_ids,
    populations,
    visc_class,
    fluid_mask,
    tau_table,
):
    groups = sizes[1] * sizes[2]
    verts = offsets.shape[1]
    hbm = pl.BlockSpec(memory_space=pltpu.HBM)
    results = pl.pallas_call(
        functools.partial(kernel, sizes),
        out_shape=(
            jax.ShapeDtypeStruct(populations.shape, F32),
            jax.ShapeDtypeStruct((groups, 4, CAP), F32),
            jax.ShapeDtypeStruct((1, verts), F32),
            jax.ShapeDtypeStruct((1, verts), I32),
        ),
        in_specs=[hbm] * 9,
        out_specs=[hbm] * 4,
        scratch_shapes=[
            pltpu.VMEM((3, verts), F32),
            pltpu.VMEM((3, verts), F32),
            pltpu.VMEM((1, verts), F32),
            pltpu.VMEM((1, verts), I32),
            pltpu.VMEM((1, verts), I32),
            pltpu.SMEM((4,), F32),
            pltpu.VMEM((19, BX, BY, BZ), F32),
            pltpu.VMEM((BX, BY, BZ), I32),
            pltpu.VMEM((BX, BY, BZ), I32),
            pltpu.VMEM((1, verts), F32),
            pltpu.VMEM((1, verts), I32),
            pltpu.VMEM((16, verts), F32),
            pltpu.VMEM((CAP, verts), BF16),
            pltpu.VMEM((groups * 16, verts), BF16),
            pltpu.VMEM((groups, 8, CAP), F32),
            pltpu.VMEM((groups, 8, CAP), F32),
            [pltpu.VMEM((TZ, count * CAP), F32) for count in PARTS],
            [pltpu.VMEM((2 * SITES, count * CAP), BF16) for count in PARTS],
            [pltpu.VMEM((6 * BZ, count * CAP), BF16) for count in PARTS],
            pltpu.VMEM((2 * SITES, 6 * BZ), F32),
            pltpu.VMEM((3 * SITES, BZ), F32),
            pltpu.VMEM((19 * XPAD * YPAD, BZ), F32),
            pltpu.VMEM((19 * XPAD * YPAD, BZ), F32),
            pltpu.VMEM((2, 2, 5, BY, BZ), F32),
            pltpu.VMEM((2, 2, 5, BY, BZ), F32),
            pltpu.VMEM((2, 2, 5, BX, BZ), F32),
            pltpu.VMEM((2, 2, 5, BX, BZ), F32),
            pltpu.VMEM((2, 2, 2, BX, BZ), F32),
            pltpu.VMEM((2, BY, 128), F32),
            pltpu.VMEM((2, BY, 128), F32),
            pltpu.VMEM((2, 2, BY, 128), F32),
            pltpu.VMEM((2, 2, 2, BY, 128), F32),
            pltpu.VMEM((2, 2, 2, 8, 128), F32),
            pltpu.VMEM((2, YPAD, 128), F32),
            pltpu.VMEM((3 * SITES, BZ), F32),
            pltpu.VMEM((19, BX, BY, BZ), F32),
            pltpu.VMEM((25, BX, BY, BZ), F32),
            pltpu.VMEM((groups, 4, CAP), F32),
            pltpu.SemaphoreType.DMA((9,)),
            pltpu.SemaphoreType.DMA((4,)),
            pltpu.SemaphoreType.DMA((groups,)),
            pltpu.SemaphoreType.DMA((groups,)),
            pltpu.SemaphoreType.DMA((2, 18)),
            pltpu.SemaphoreType.DMA((2, 18)),
            pltpu.SemaphoreType.DMA((groups,)),
            pltpu.SemaphoreType.DMA((groups,)),
        ],
        compiler_params=pltpu.CompilerParams(
            collective_id=0, has_side_effects=True, vmem_limit_bytes=60 * 1024 * 1024
        ),
    )(
        offsets,
        anchor,
        stiffness.reshape(1, verts),
        lattice_block.reshape(1, verts),
        tile_ids.reshape(1, verts),
        tau_table,
        populations,
        visc_class,
        fluid_mask,
    )
    return pl.pallas_call(
        hand_over,
        out_shape=[
            jax.ShapeDtypeStruct(populations.shape, F32),
            jax.ShapeDtypeStruct((3, verts), F32),
        ],
        in_specs=[hbm] * 4,
        out_specs=[hbm] * 2,
        scratch_shapes=[
            pltpu.VMEM(populations.shape, F32),
            pltpu.VMEM((groups, 4, CAP), F32),
            pltpu.VMEM((1, verts), F32),
            pltpu.VMEM((1, verts), I32),
            pltpu.VMEM((3, verts), F32),
            pltpu.SemaphoreType.DMA((3 + len(PIECES),)),
            pltpu.SemaphoreType.DMA((len(PIECES) + 1,)),
        ],
        compiler_params=pltpu.CompilerParams(vmem_limit_bytes=60 * 1024 * 1024),
    )(*results)


def solution(mesh):
    placed = (
        P(None, ("gx", "gy", "gz")),
        P(None, ("gx", "gy", "gz")),
        P(("gx", "gy", "gz")),
        P(("gx", "gy", "gz"), None),
        P(("gx", "gy", "gz")),
        P(None, "gx", "gy", "gz"),
        P("gx", "gy", "gz"),
        P("gx", "gy", "gz"),
        P(),
    )
    sizes = tuple(mesh.shape[axis] for axis in ("gx", "gy", "gz"))
    return jax.shard_map(
        functools.partial(on_device, sizes),
        mesh=mesh,
        in_specs=placed,
        out_specs=(P(None, "gx", "gy", "gz"), P(None, ("gx", "gy", "gz"))),
        check_vma=False,
    )
```
